256 devices in a mesh: patch: 16 (over z, core), visit: 16 (over y, x).
Axes of the slice: x: 4, y: 4, z: 8, core: 2. Of those that a mesh axis runs over, the one named last changes fastest.
Arguments:
- blocks: bfloat16 [16, 16, 16, 256, 256], P('patch', 'visit'), may hold values from -6 to 6
- block_patch: int32 [16, 16, 16, 1], P('patch', 'visit'), may hold values from 0 to 15; in each aligned block of 16 rows (0 to 15, 16 to 31, ..., all dimensions but the last counted through in order) at most 2 rows name the same one
- block_slot: int32 [16, 16, 16], P('patch', 'visit'), may hold values from 0 to 7
- block_count: int32 [16, 16], P('patch', 'visit'), may hold values from 12 to 16, as said below
- template: bfloat16 [16, 512, 1024], P('patch', 'visit'), may hold values from -6 to 6
- basis_rows: bfloat16 [9, 21], replicated, may hold values from -1.25 to 1.25
- basis_cols: float32 [9, 21], replicated, may hold values from -1.25 to 1.25
- coeffs: float32 [16, 9], P('visit'), may hold values from -2 to 2
- psf_rows: bfloat16 [16, 2, 25], P('visit'), may hold values from -1.25 to 1.25
- psf_cols: bfloat16 [16, 2, 25], P('visit'), may hold values from -1.25 to 1.25
Outputs:
- filtered: float32 [16, 16, 512, 1024], P('patch', 'visit')
The draws below stay inside these ranges and needn't reach their ends.
Inputs may be any that keep to these rules, and one draw needn't show every extreme that they name: `block_patch`: among the 16 entries of one list (one patch index and visit) no patch is named more than 2 times, and some list names a patch exactly 2 times. Entries at positions block_count and beyond are unused.
All inputs are finite; a program needn't handle non-finite values.
Results may differ from the reference program's by a relative error of at most 0.005.
Values may be sent and summed in bfloat16 or wider, within the bound.
No kernel may reach another device: no remote copies, remote signals or barrier semaphores. Data moves between devices by JAX's collectives and lax.ppermute only.
A program may use at most 128 MiB of HBM per device.

```python
import math
import jax
import jax.numpy as jnp
import numpy as np
from jax import lax

BLK = 256
PATCH_ROWS = 512
PATCH_COLS = 1024
NB_DEV = 16
CAP = 2
NBASIS = 9
KBASIS = 21
KPSF = 25
NPSF = 2
SLOTS = 8
N_PATCH = 16
N_VISIT = 16


def draw_block_count(key, part):
    counts = jax.random.randint(key, (N_PATCH, N_VISIT), 3 * NB_DEV // 4, NB_DEV + 1)
    counts = counts.at[0, 0].set(NB_DEV)
    counts = counts.at[N_PATCH - 1, N_VISIT - 1].set(3 * NB_DEV // 4)
    return counts.astype(jnp.int32)


def plant(array, rng, smallest, high):
    index_at = [jax.random.randint(jax.random.fold_in(rng, axis), (), 0, length) for axis, length in enumerate(array.shape)]
    longest = array.shape.index(max(array.shape))
    beside = index_at[:longest] + [(index_at[longest] + 1) % array.shape[longest]] + index_at[longest + 1:]
    return array.at[tuple(index_at)].set(smallest).at[tuple(beside)].set(high)


def steps_of(rng, dims, split, least, high):
    factor_of = 1.0
    for position, blocks in split:
        draws = jax.random.uniform(jax.random.fold_in(jax.random.fold_in(rng, 6), position), (blocks,), jnp.float32, least / len(split), high / len(split))
        factor_of = factor_of * jnp.repeat(jnp.exp(draws), dims[position] // blocks).reshape((-1,) + (1,) * (len(dims) - 1 - position))
    return factor_of


def assign_block(own_key, own, number, rows, amount, top, limit, lean):
    order = jax.random.permutation(own_key, amount)
    crowded, ordinary = shares(amount, rows * top, limit, lean, True), shares(amount, rows * top, limit, lean, False)
    places = jnp.arange(amount)

    def named(sizes, offset_by):
        used = int((sizes > 0).sum())
        fixed = max(1, used // 4)
        shifted = fixed + (places - fixed + offset_by * (used - fixed)) % max(1, amount - fixed)
        return jnp.zeros((amount,), jnp.int32).at[order[jnp.where(places < fixed, places, shifted)]].set(jnp.asarray(sizes, jnp.int32))

    sizes = jnp.where(number % 4 == 0, named(crowded, number // 4), named(ordinary, number - number // 4 - 1))
    mixed = jax.random.permutation(jax.random.fold_in(own, 3), amount)
    giver, taker = mixed[0:amount // 2 * 2:2], mixed[1:amount // 2 * 2:2]
    slack = jnp.minimum(sizes[giver] - 1, limit - sizes[taker]) // 2
    slack = jnp.where((giver == order[0]) | (taker == order[0]) | (sizes[taker] == 0), 0, jnp.maximum(slack, 0))
    shifted = jax.random.randint(jax.random.fold_in(own, 4), (amount // 2,), 0, 1 << 20) % (slack + 1)
    sizes = sizes.at[giver].add(-shifted).at[taker].add(shifted)
    labels = jnp.searchsorted(jnp.cumsum(sizes), jnp.arange(rows * top), side="right").astype(jnp.int32)
    listing = labels.reshape(top, rows).T
    listing = listing[jax.random.permutation(jax.random.fold_in(own, 1), rows)]
    offset_by = jax.random.randint(jax.random.fold_in(own, 2), (rows, 1), 0, top)
    return jnp.take_along_axis(listing, (jnp.arange(top)[None, :] + offset_by) % top, axis=1)


def shares(count, total, bound, skew, full):
    loads = [(1 << 20) // math.isqrt(grade ** skew) + 1 for grade in range(1, count + 1)]
    largest = bound if full else min(bound, max(-(-total // count), total * loads[0] // sum(loads)))
    least = 1 if total - largest >= count - 1 else 0
    given, rest = [largest] + [least] * (count - 1), total - largest - least * (count - 1)
    while rest > 0:
        free = [i for i in range(1, count) if given[i] < largest] or [i for i in range(1, count) if given[i] < bound]
        mass, remaining = sum([loads[i] for i in free]), rest
        for i in free:
            addition = min(bound - given[i], max(1, remaining * loads[i] // mass), rest)
            given[i] = given[i] + addition
            rest = rest - addition
    return np.array(given)


def noise(rng, shape, scale, most, shards=(), held_as=jnp.bfloat16):
    values = scale * jax.random.normal(rng, shape, jnp.float32)
    if shards:
        values = values * steps_of(rng, shape, shards, -0.22, 0.18)
    return jnp.clip(values, -most, most).astype(held_as)


def setup_inputs(seed: int = 0) -> dict:
    seeds = jax.random.split(jax.random.key(seed), 11)
    blocks = noise(seeds[0], (N_PATCH, N_VISIT, NB_DEV, BLK, BLK), 1.0, 6.0, ((0, 16), (1, 16)))
    block_patch_keys = jax.random.split(jax.random.fold_in(seeds[1], 1), N_PATCH * N_VISIT * NB_DEV // NB_DEV)
    block_patch_turns = jax.random.permutation(jax.random.fold_in(seeds[1], 3), N_PATCH * N_VISIT * NB_DEV // NB_DEV)
    block_patch = jax.vmap(lambda own, number: assign_block(jax.random.fold_in(seeds[1], 2), own, number, NB_DEV, N_PATCH, 1, CAP, 2))(block_patch_keys, block_patch_turns).reshape((N_PATCH, N_VISIT, NB_DEV, 1))
    block_slot = plant(jax.random.randint(seeds[2], (N_PATCH, N_VISIT, NB_DEV), 0, SLOTS), jax.random.fold_in(seeds[2], 1), 0, SLOTS - 1).astype(jnp.int32)
    block_count = draw_block_count(jax.random.fold_in(seeds[10], 71), 0)
    template = noise(seeds[4], (N_PATCH, PATCH_ROWS, PATCH_COLS), 1.0, 6.0, ((0, 16), (1, 16)))
    basis_rows = noise(seeds[5], (NBASIS, KBASIS), KBASIS ** -0.5, 1.25)
    basis_cols = noise(seeds[6], (NBASIS, KBASIS), KBASIS ** -0.5, 1.25, (), jnp.float32)
    coeffs = noise(seeds[7], (N_VISIT, NBASIS), 0.33, 2.0, ((0, 16),), jnp.float32)
    psf_rows = noise(seeds[8], (N_VISIT, NPSF, KPSF), KPSF ** -0.5, 1.25, ((0, 16),))
    psf_cols = noise(seeds[9], (N_VISIT, NPSF, KPSF), KPSF ** -0.5, 1.25, ((0, 16),))
    return {"blocks": blocks, "block_patch": block_patch, "block_slot": block_slot, "block_count": block_count, "template": template, "basis_rows": basis_rows, "basis_cols": basis_cols, "coeffs": coeffs, "psf_rows": psf_rows, "psf_cols": psf_cols}


def rounded(values):
    return lax.optimization_barrier(values.astype(jnp.bfloat16)).astype(jnp.float32)


def correlate(source, kernel_taps, along_axis):
    length = kernel_taps.shape[-1]
    half_len = length // 2
    extent = source.shape[along_axis]
    padding = [(0, 0)] * source.ndim
    padding[along_axis] = (half_len, half_len)
    padded = jnp.pad(source, padding)
    summed = jnp.zeros(source.shape, jnp.float32)
    for offset in range(length):
        summed = summed + kernel_taps[:, offset][:, None, None] * lax.slice_in_dim(padded, offset, offset + extent, axis=along_axis)
    return summed


def reference(blocks, block_patch, block_slot, block_count, template, basis_rows, basis_cols, coeffs, psf_rows, psf_cols):
    tall_count = PATCH_ROWS // BLK
    wide_count = PATCH_COLS // BLK
    live_mask = jnp.arange(NB_DEV, dtype=jnp.int32)[None, None, :] < block_count[:, :, None]
    destination = block_patch[..., 0]
    row_taps = basis_rows.astype(jnp.float32)

    def one_patch(patch_id):
        source = jnp.broadcast_to(template[patch_id].astype(jnp.float32)[None], (NBASIS, PATCH_ROWS, PATCH_COLS))
        smoothed = rounded(correlate(source, row_taps, 2))

        def one_visit(visit_id):
            chosen = live_mask[:, visit_id] & (destination[:, visit_id] == patch_id)
            segment_ids = jnp.where(chosen, block_slot[:, visit_id], SLOTS).reshape(-1).astype(jnp.int32)
            pieces = blocks[:, visit_id].astype(jnp.float32).reshape(N_PATCH * NB_DEV, BLK * BLK)
            slot_images = jax.ops.segment_sum(pieces, segment_ids, num_segments=SLOTS)
            science = slot_images.reshape(tall_count, wide_count, BLK, BLK).transpose(0, 2, 1, 3).reshape(PATCH_ROWS, PATCH_COLS)
            scaled = rounded(coeffs[visit_id][:, None] * basis_cols)
            model_image = jnp.sum(correlate(smoothed, scaled, 1), axis=0)
            difference = rounded(science - model_image)
            spread = jnp.broadcast_to(difference[None], (NPSF, PATCH_ROWS, PATCH_COLS))
            blurred = rounded(correlate(spread, psf_rows[visit_id].astype(jnp.float32), 2))
            return jnp.sum(correlate(blurred, psf_cols[visit_id].astype(jnp.float32), 1), axis=0)

        return lax.map(one_visit, jnp.arange(N_VISIT, dtype=jnp.int32))

    return lax.map(one_patch, jnp.arange(N_PATCH, dtype=jnp.int32))
```

```python
import jax
import jax.numpy as jnp
from jax import lax
from jax.experimental import pallas as pl
from jax.experimental.pallas import tpu as pltpu
from jax.sharding import PartitionSpec as P

CAP = 2
LANE = 128
HALO = 64
WINDOW = 256
LAP = 16
F32 = jnp.float32
BF16 = jnp.bfloat16
PARAMS = pltpu.CompilerParams(vmem_limit_bytes=48 * 1024 * 1024)
SMEM = pl.BlockSpec(memory_space=pltpu.SMEM)
VMEM = pl.BlockSpec(memory_space=pltpu.VMEM)
ANY = pl.BlockSpec(memory_space=pl.ANY)


def pack_kernel(patch, slot, count, blocks, outgoing, labels, place, sems):
    entries, edge = blocks.shape[0], blocks.shape[1]
    for row in range(labels.shape[0]):
        for copy in range(CAP):
            labels[row, copy] = -1
    used = jnp.minimum(count[0], entries)

    def send(i, carry):
        target = patch[i]
        copy = jnp.where(labels[target, 0] < 0, 0, 1)
        labels[target, copy] = slot[i]
        place[i] = copy
        move(i, target, copy).start()
        return carry

    def move(i, target, copy):
        start = pl.multiple_of(copy * edge, edge)
        return pltpu.make_async_copy(
            blocks.at[i], outgoing.at[target, pl.ds(start, edge)], sems.at[i]
        )

    def finish(i, carry):
        move(i, patch[i], place[i]).wait()
        return carry

    lax.fori_loop(0, used, send, 0)
    lax.fori_loop(0, used, finish, 0)


def pack(blocks, block_patch, block_slot, block_count, places):
    entries, edge, _ = blocks.shape
    return pl.pallas_call(
        pack_kernel,
        out_shape=(
            jax.ShapeDtypeStruct((places, CAP * edge, edge), blocks.dtype),
            jax.ShapeDtypeStruct((places, CAP), jnp.int32),
        ),
        in_specs=[SMEM, SMEM, SMEM, ANY],
        out_specs=(ANY, SMEM),
        scratch_shapes=[pltpu.SMEM((entries,), jnp.int32), pltpu.SemaphoreType.DMA((entries,))],
        compiler_params=PARAMS,
        name="pack",
    )(block_patch, block_slot, block_count, blocks)


def fill_band(table, taps, index, row0, col0, height, breadth, sign, base):
    length = taps.shape[1]
    for r in range(0, height, 16):
        rows = lax.broadcasted_iota(jnp.int32, (16, breadth), 0)
        cols = lax.broadcasted_iota(jnp.int32, (16, breadth), 1)
        offset = sign * (rows - cols) + (sign * r + base)
        values = jnp.zeros((16, breadth), F32)
        for u in range(length):
            values = jnp.where(offset == u, taps[index, u], values)
        table[pl.ds(row0 + r, 16), pl.ds(col0, breadth)] = values.astype(table.dtype)


def fill_tables(col_table, row_table, col_taps, row_taps):
    half = col_taps.shape[1] // 2
    for k in range(col_taps.shape[0]):
        fill_band(col_table, col_taps, k, 0, k * LANE, WINDOW, LANE, 1, half - HALO)
        for w in range(2):
            fill_band(
                row_table.at[w], row_taps, k, 0, k * WINDOW, WINDOW + LAP, WINDOW, -1,
                half + w * LAP,
            )


def shifted(values):
    rows = values.shape[0]
    edge = jnp.zeros((rows, HALO), F32)
    return jnp.concatenate([edge, values, edge], axis=1).astype(BF16)


def filter_strip(padded, col_table, row_table, stage, strip):
    count = col_table.shape[1] // LANE
    for h in range(2):
        start = strip * WINDOW + h * LANE
        if not isinstance(start, int):
            start = pl.multiple_of(start, LANE)
        for w in range(2):
            across = jnp.dot(
                padded[pl.ds(w * WINDOW, WINDOW), pl.ds(start, WINDOW)],
                col_table[...],
                preferred_element_type=F32,
            ).astype(BF16)
            for k in range(count):
                stage[w, pl.ds(k * WINDOW, WINDOW), pl.ds(h * LANE, LANE)] = across[
                    :, k * LANE : (k + 1) * LANE
                ]
    top = jnp.dot(row_table[0], stage[0], preferred_element_type=F32)
    low = jnp.dot(row_table[1], stage[1], preferred_element_type=F32)
    cut = WINDOW - LAP
    return top[:cut], top[cut:] + low[: 2 * LAP], low[2 * LAP :]


def store_strip(target, parts, strip):
    start = strip * WINDOW
    if not isinstance(start, int):
        start = pl.multiple_of(start, LANE)
    row = 0
    for part in parts:
        target[pl.ds(row, part.shape[0]), pl.ds(start, WINDOW)] = part
        row += part.shape[0]


def make_model(pieces, me, basis_rows, scaled, psf_rows, psf_cols):
    parts = len(pieces)
    local_rows, breadth = pieces[0].shape
    height = parts * local_rows
    basis, components = basis_rows.shape[0], psf_rows.shape[0]

    def kernel(*refs):
        sources = refs[:parts]
        (position, basis_taps, scaled_taps, psf_row_taps, psf_col_taps, model, psf_col_table,
         psf_row_table, padded, col_table, row_table, stage) = refs[parts:]
        fill_tables(col_table, row_table, basis_taps, scaled_taps)
        for d, source in enumerate(sources):
            owner = lax.rem(position[0] - d + parts, parts)
            padded[pl.ds(pl.multiple_of(owner * local_rows, local_rows), local_rows), :] = shifted(
                source[...].astype(F32)
            )

        def strip(j, carry):
            store_strip(model, filter_strip(padded, col_table, row_table, stage, j), j)
            return carry

        lax.fori_loop(0, breadth // WINDOW, strip, 0)
        fill_tables(psf_col_table, psf_row_table, psf_row_taps, psf_col_taps)

    return pl.pallas_call(
        kernel,
        out_shape=(
            jax.ShapeDtypeStruct((height, breadth), F32),
            jax.ShapeDtypeStruct((WINDOW, components * LANE), BF16),
            jax.ShapeDtypeStruct((2, WINDOW + LAP, components * WINDOW), BF16),
        ),
        in_specs=[VMEM] * parts + [SMEM] * 5,
        out_specs=(VMEM, VMEM, VMEM),
        scratch_shapes=[
            pltpu.VMEM((height, breadth + 2 * HALO), BF16),
            pltpu.VMEM((WINDOW, basis * LANE), BF16),
            pltpu.VMEM((2, WINDOW + LAP, basis * WINDOW), BF16),
            pltpu.VMEM((2, basis * WINDOW, WINDOW), BF16),
        ],
        compiler_params=PARAMS,
        name="model",
    )(*pieces, me, basis_rows, scaled, psf_rows, psf_cols)


def finish_kernel(labels, arrived, model, col_table, row_table, out, held, total, padded, stage,
                  result, sems, out_sems):
    sources = labels.shape[0]
    edge = held.shape[1]
    height, breadth = total.shape
    wide = breadth // edge

    def fetch(t):
        p, c = lax.div(t, CAP), lax.rem(t, CAP)
        start = pl.multiple_of(c * edge, edge)
        copy = pltpu.make_async_copy(arrived.at[p, pl.ds(start, edge)], held.at[t], sems.at[t])
        return labels[p, c], copy

    def begin(t, carry):
        label, copy = fetch(t)

        @pl.when(label >= 0)
        def _():
            copy.start()

        return carry

    def add(t, carry):
        label, copy = fetch(t)

        @pl.when(label >= 0)
        def _():
            copy.wait()
            row = pl.multiple_of(lax.div(label, wide) * edge, edge)
            col = pl.multiple_of(lax.rem(label, wide) * edge, edge)
            here = (pl.ds(row, edge), pl.ds(col, edge))
            total[here] = total[here] + held[t].astype(F32)

        return carry

    lax.fori_loop(0, sources * CAP, begin, 0)
    total[...] = -model[...]
    lax.fori_loop(0, sources * CAP, add, 0)
    for r in range(0, height, LANE):
        padded[pl.ds(r, LANE), :] = shifted(total[pl.ds(r, LANE), :])
    copies = []
    for j in range(breadth // WINDOW):
        store_strip(result, filter_strip(padded, col_table, row_table, stage, j), j)
        here = (pl.ds(0, height), pl.ds(j * WINDOW, WINDOW))
        copies.append(pltpu.make_async_copy(result.at[here], out.at[here], out_sems.at[j]))
        copies[-1].start()
    for copy in copies:
        copy.wait()


def finish(labels, arrived, model, col_table, row_table):
    height, breadth = model.shape
    sources, edge = labels.shape[0], arrived.shape[2]
    components = col_table.shape[1] // LANE
    return pl.pallas_call(
        finish_kernel,
        out_shape=jax.ShapeDtypeStruct((height, breadth), F32),
        in_specs=[SMEM, ANY, VMEM, VMEM, VMEM],
        out_specs=ANY,
        scratch_shapes=[
            pltpu.VMEM((sources * CAP, edge, edge), BF16),
            pltpu.VMEM((height, breadth), F32),
            pltpu.VMEM((height, breadth + 2 * HALO), BF16),
            pltpu.VMEM((2, components * WINDOW, WINDOW), BF16),
            pltpu.VMEM((height, breadth), F32),
            pltpu.SemaphoreType.DMA((sources * CAP,)),
            pltpu.SemaphoreType.DMA((breadth // WINDOW,)),
        ],
        compiler_params=PARAMS,
        name="finish",
    )(labels, arrived, model, col_table, row_table)


def per_device(
    blocks,
    block_patch,
    block_slot,
    block_count,
    template,
    basis_rows,
    basis_cols,
    coeffs,
    psf_rows,
    psf_cols,
):
    n_patch, n_visit = lax.axis_size("patch"), lax.axis_size("visit")
    outgoing, labels = pack(
        blocks[0, 0],
        block_patch.reshape(-1),
        block_slot.reshape(-1),
        block_count.reshape(-1),
        n_patch,
    )
    arrived_labels = lax.all_to_all(labels, "patch", 0, 0, tiled=True)
    arrived = lax.all_to_all(outgoing, "patch", 0, 0, tiled=True)
    rows = template[0]
    pieces = [rows]
    for d in range(1, n_visit):
        ring = [(i, (i + d) % n_visit) for i in range(n_visit)]
        pieces.append(lax.ppermute(rows, "visit", ring))
    scaled = coeffs[0][:, None] * basis_cols
    me = lax.axis_index("visit").reshape(1).astype(jnp.int32)
    model, col_table, row_table = make_model(
        pieces, me, basis_rows.astype(F32), scaled, psf_rows[0].astype(F32),
        psf_cols[0].astype(F32),
    )
    filtered = finish(arrived_labels, arrived, model, col_table, row_table)
    return filtered[None, None]


def solution(mesh):
    placed = (
        P("patch", "visit", None, None, None),
        P("patch", "visit", None, None),
        P("patch", "visit", None),
        P("patch", "visit"),
        P("patch", "visit", None),
        P(),
        P(),
        P("visit", None),
        P("visit", None, None),
        P("visit", None, None),
    )
    return jax.shard_map(
        per_device,
        mesh=mesh,
        in_specs=placed,
        out_specs=P("patch", "visit", None, None),
        check_vma=False,
    )
```

```python
import jax
import jax.numpy as jnp
from jax import lax
from jax.experimental import pallas as pl
from jax.experimental.pallas import tpu as pltpu
from jax.sharding import PartitionSpec as P

CORES = 2
NOTE_ROWS = 16
NOTE_WORDS = 8
LANE = 128
HALO = 64
WINDOW = 256
LAP = 16
F32 = jnp.float32
BF16 = jnp.bfloat16
PARAMS = pltpu.CompilerParams(vmem_limit_bytes=48 * 1024 * 1024)
SMEM = pl.BlockSpec(memory_space=pltpu.SMEM)
VMEM = pl.BlockSpec(memory_space=pltpu.VMEM)
HBM = pl.BlockSpec(memory_space=pltpu.HBM)


def scan_entries(lists, first, second, extra, chips, here):
    patch, count, entries = lists
    for q in range(first.shape[0]):
        first[q] = -1
        second[q] = -1
    for d in range(chips):
        extra[d] = -1

    def visit(i, left_over):
        q = patch[i]
        again = first[q] >= 0
        d = lax.rem(lax.div(q, CORES) - here + chips, chips)
        taken = extra[d] >= 0

        @pl.when(jnp.logical_not(again))
        def _():
            first[q] = i

        @pl.when(again)
        def _():
            second[q] = i

        @pl.when(jnp.logical_and(again, jnp.logical_not(taken)))
        def _():
            extra[d] = i

        return left_over + jnp.logical_and(again, taken).astype(jnp.int32)

    return lax.fori_loop(0, jnp.minimum(count[0], entries), visit, jnp.int32(0))


def load_lists(sources, targets, sems):
    copies = [
        pltpu.make_async_copy(source, target, sems.at[n])
        for n, (source, target) in enumerate(zip(sources, targets))
    ]
    for copy in copies:
        copy.start()
    for copy in copies:
        copy.wait()


def run_copies(copies):
    for wanted, copy in copies:
        pl.when(wanted)(copy.start)
    for wanted, copy in copies:
        pl.when(wanted)(copy.wait)


def pack_extra_kernel(patch_in, count_in, blocks, after, *refs):
    chips = len(refs) - 7
    outs = refs[:chips]
    patch, count, first, second, extra, list_sems, sems = refs[chips:]
    load_lists((patch_in, count_in), (patch, count), list_sems)
    here = lax.div(lax.axis_index("patch"), CORES)
    scan_entries((patch, count, blocks.shape[0]), first, second, extra, chips, here)
    copies = []
    for d in range(chips):
        i = extra[d]
        copy = pltpu.make_async_copy(blocks.at[jnp.maximum(i, 0)], outs[d], sems.at[d])
        copies.append((i >= 0, copy))
    run_copies(copies)


def pack_extra(blocks, block_patch, block_count, after, places):
    entries, edge, _ = blocks.shape
    chips = places // CORES
    return pl.pallas_call(
        pack_extra_kernel,
        out_shape=(jax.ShapeDtypeStruct((edge, edge), blocks.dtype),) * chips,
        in_specs=[HBM] * 4,
        out_specs=(HBM,) * chips,
        scratch_shapes=[
            pltpu.SMEM((entries,), jnp.int32),
            pltpu.SMEM((1,), jnp.int32),
            pltpu.SMEM((places,), jnp.int32),
            pltpu.SMEM((places,), jnp.int32),
            pltpu.SMEM((chips,), jnp.int32),
            pltpu.SemaphoreType.DMA((2,)),
            pltpu.SemaphoreType.DMA((chips,)),
        ],
        compiler_params=PARAMS,
        name="pack_extra",
    )(block_patch, block_count, blocks, after)


def pack_main_kernel(patch_in, slot_in, count_in, blocks, outgoing, patch, slot, count,
                     first, second, extra, notes, list_sems, sems, note_sem):
    places = outgoing.shape[0]
    edge = blocks.shape[1]
    chips = places // CORES
    load_lists((patch_in, slot_in, count_in), (patch, slot, count), list_sems)
    here = lax.div(lax.axis_index("patch"), CORES)
    left_over = scan_entries((patch, count, blocks.shape[0]), first, second, extra, chips, here)
    copies = []
    for q in range(places):
        i = first[q]
        copy = pltpu.make_async_copy(
            blocks.at[jnp.maximum(i, 0)], outgoing.at[q, pl.ds(0, edge)], sems.at[q]
        )
        copies.append((i >= 0, copy))
    for wanted, copy in copies:
        pl.when(wanted)(copy.start)
    lane = lax.broadcasted_iota(jnp.int32, (NOTE_ROWS, edge), 1)
    for q in range(places):
        i, j = first[q], second[q]
        e = extra[lax.rem(q // CORES - here + chips, chips)]
        words = (
            jnp.where(i >= 0, slot[jnp.maximum(i, 0)], -1),
            jnp.where(e >= 0, lax.rem(patch[jnp.maximum(e, 0)], CORES), -1),
            jnp.where(e >= 0, slot[jnp.maximum(e, 0)], -1),
            left_over,
            jnp.where(j >= 0, slot[jnp.maximum(j, 0)], -1),
        )
        row = jnp.zeros((NOTE_ROWS, edge), jnp.int32)
        for n, word in enumerate(words):
            row = jnp.where(lane == n, word, row)
        notes[q] = row.astype(F32).astype(notes.dtype)
    note_copy = pltpu.make_async_copy(notes, outgoing.at[:, pl.ds(edge, NOTE_ROWS)], note_sem)
    note_copy.start()
    for wanted, copy in copies:
        pl.when(wanted)(copy.wait)
    note_copy.wait()


def pack_main(blocks, block_patch, block_slot, block_count, places):
    entries, edge, _ = blocks.shape
    return pl.pallas_call(
        pack_main_kernel,
        out_shape=jax.ShapeDtypeStruct((places, edge + NOTE_ROWS, edge), blocks.dtype),
        in_specs=[HBM] * 4,
        out_specs=HBM,
        scratch_shapes=[
            pltpu.SMEM((entries,), jnp.int32),
            pltpu.SMEM((entries,), jnp.int32),
            pltpu.SMEM((1,), jnp.int32),
            pltpu.SMEM((places,), jnp.int32),
            pltpu.SMEM((places,), jnp.int32),
            pltpu.SMEM((places // CORES,), jnp.int32),
            pltpu.VMEM((places, NOTE_ROWS, edge), blocks.dtype),
            pltpu.SemaphoreType.DMA((3,)),
            pltpu.SemaphoreType.DMA((places,)),
            pltpu.SemaphoreType.DMA,
        ],
        compiler_params=PARAMS,
        name="pack_main",
    )(block_patch, block_slot, block_count, blocks)


def pack_second_kernel(patch_in, count_in, blocks, outgoing, patch, count, first, second, extra,
                       list_sems, sems):
    places = outgoing.shape[0]
    chips = places // CORES
    load_lists((patch_in, count_in), (patch, count), list_sems)
    here = lax.div(lax.axis_index("patch"), CORES)
    scan_entries((patch, count, blocks.shape[0]), first, second, extra, chips, here)
    copies = []
    for q in range(places):
        i = second[q]
        copy = pltpu.make_async_copy(blocks.at[jnp.maximum(i, 0)], outgoing.at[q], sems.at[q])
        copies.append((i >= 0, copy))
    run_copies(copies)


def pack_second(blocks, block_patch, block_count, places):
    entries, edge, _ = blocks.shape
    return pl.pallas_call(
        pack_second_kernel,
        out_shape=jax.ShapeDtypeStruct((places, edge, edge), blocks.dtype),
        in_specs=[HBM] * 3,
        out_specs=HBM,
        scratch_shapes=[
            pltpu.SMEM((entries,), jnp.int32),
            pltpu.SMEM((1,), jnp.int32),
            pltpu.SMEM((places,), jnp.int32),
            pltpu.SMEM((places,), jnp.int32),
            pltpu.SMEM((places // CORES,), jnp.int32),
            pltpu.SemaphoreType.DMA((2,)),
            pltpu.SemaphoreType.DMA((places,)),
        ],
        compiler_params=PARAMS,
        name="pack_second",
    )(block_patch, block_count, blocks)


def fill_band(table, taps, index, row0, col0, height, breadth, sign, base):
    length = taps.shape[1]
    for r in range(0, height, 16):
        rows = lax.broadcasted_iota(jnp.int32, (16, breadth), 0)
        cols = lax.broadcasted_iota(jnp.int32, (16, breadth), 1)
        offset = sign * (rows - cols) + (sign * r + base)
        values = jnp.zeros((16, breadth), F32)
        for u in range(length):
            values = jnp.where(offset == u, taps[index, u], values)
        table[pl.ds(row0 + r, 16), pl.ds(col0, breadth)] = values.astype(table.dtype)


def fill_tables(col_table, row_table, col_taps, row_taps):
    half = col_taps.shape[1] // 2
    for k in range(col_taps.shape[0]):
        fill_band(col_table, col_taps, k, 0, k * LANE, WINDOW, LANE, 1, half - HALO)
        for w in range(2):
            fill_band(
                row_table.at[w], row_taps, k, 0, k * WINDOW, WINDOW + LAP, WINDOW, -1,
                half + w * LAP,
            )


def shifted(values):
    rows = values.shape[0]
    edge = jnp.zeros((rows, HALO), F32)
    return jnp.concatenate([edge, values, edge], axis=1).astype(BF16)


def filter_strip(padded, col_table, row_table, stage, strip):
    count = col_table.shape[1] // LANE
    for h in range(2):
        start = strip * WINDOW + h * LANE
        if not isinstance(start, int):
            start = pl.multiple_of(start, LANE)
        for w in range(2):
            across = jnp.dot(
                padded[pl.ds(w * WINDOW, WINDOW), pl.ds(start, WINDOW)],
                col_table[...],
                preferred_element_type=F32,
            ).astype(BF16)
            for k in range(count):
                stage[w, pl.ds(k * WINDOW, WINDOW), pl.ds(h * LANE, LANE)] = across[
                    :, k * LANE : (k + 1) * LANE
                ]
    top = jnp.dot(row_table[0], stage[0], preferred_element_type=F32)
    low = jnp.dot(row_table[1], stage[1], preferred_element_type=F32)
    cut = WINDOW - LAP
    return top[:cut], top[cut:] + low[: 2 * LAP], low[2 * LAP :]


def store_strip(target, parts, strip):
    start = strip * WINDOW
    if not isinstance(start, int):
        start = pl.multiple_of(start, LANE)
    row = 0
    for part in parts:
        target[pl.ds(row, part.shape[0]), pl.ds(start, WINDOW)] = part
        row += part.shape[0]


def make_model(pieces, me, basis_rows, scaled, psf_rows, psf_cols):
    parts = len(pieces)
    group_rows, breadth = pieces[0].shape
    local_rows = group_rows // parts
    height = parts * group_rows
    basis, components = basis_rows.shape[0], psf_rows.shape[0]

    def kernel(*refs):
        sources = refs[:parts]
        (position, basis_taps, scaled_taps, psf_row_taps, psf_col_taps, model, psf_col_table,
         psf_row_table, padded, col_table, row_table, stage) = refs[parts:]
        fill_tables(col_table, row_table, basis_taps, scaled_taps)
        y, x = lax.div(position[0], parts), lax.rem(position[0], parts)
        for dy, source in enumerate(sources):
            for dx in range(parts):
                owner = lax.rem(y - dy + parts, parts) * parts + lax.rem(x - dx + parts, parts)
                start = pl.multiple_of(owner * local_rows, local_rows)
                padded[pl.ds(start, local_rows), :] = shifted(
                    source[pl.ds(dx * local_rows, local_rows), :].astype(F32)
                )

        def strip(j, carry):
            store_strip(model, filter_strip(padded, col_table, row_table, stage, j), j)
            return carry

        lax.fori_loop(0, breadth // WINDOW, strip, 0)
        fill_tables(psf_col_table, psf_row_table, psf_row_taps, psf_col_taps)

    return pl.pallas_call(
        kernel,
        out_shape=(
            jax.ShapeDtypeStruct((height, breadth), F32),
            jax.ShapeDtypeStruct((WINDOW, components * LANE), BF16),
            jax.ShapeDtypeStruct((2, WINDOW + LAP, components * WINDOW), BF16),
        ),
        in_specs=[VMEM] * parts + [SMEM] * 5,
        out_specs=(VMEM, VMEM, VMEM),
        scratch_shapes=[
            pltpu.VMEM((height, breadth + 2 * HALO), BF16),
            pltpu.VMEM((WINDOW, basis * LANE), BF16),
            pltpu.VMEM((2, WINDOW + LAP, basis * WINDOW), BF16),
            pltpu.VMEM((2, basis * WINDOW, WINDOW), BF16),
        ],
        compiler_params=PARAMS,
        name="model",
    )(*pieces, me, basis_rows, scaled, psf_rows, psf_cols)


def spot_of(label, edge, wide):
    row = pl.multiple_of(lax.div(label, wide) * edge, edge)
    col = pl.multiple_of(lax.rem(label, wide) * edge, edge)
    return pl.ds(row, edge), pl.ds(col, edge)


def add_first(notes, main, model):
    height, breadth = model.shape
    places, edge = main.shape[0], main.shape[2]

    def kernel(words, blocks, model_in, total):
        total[...] = -model_in[...]

        def step(p, carry):
            label = words[p, 0]

            @pl.when(label >= 0)
            def _():
                spot = spot_of(label, edge, breadth // edge)
                total[spot] = total[spot] + blocks[p, pl.ds(0, edge), :].astype(F32)

            return carry

        lax.fori_loop(0, places, step, 0)

    return pl.pallas_call(
        kernel,
        out_shape=jax.ShapeDtypeStruct((height, breadth), F32),
        in_specs=[SMEM, VMEM, VMEM],
        out_specs=VMEM,
        compiler_params=PARAMS,
        name="add_first",
    )(notes, main, model)


def no_second(shape, dtype):
    return pl.pallas_call(
        lambda out: None,
        out_shape=jax.ShapeDtypeStruct(shape, dtype),
        out_specs=HBM,
        compiler_params=PARAMS,
        name="no_second",
    )()


def finish(notes, own, other, second, total, col_table, row_table):
    height, breadth = total.shape
    places, edge = notes.shape[0], second.shape[1]
    components = col_table.shape[1] // LANE
    chips = len(own)
    wide = breadth // edge

    def kernel(*refs):
        words, by_core = refs[0], (refs[1 : 1 + chips], refs[1 + chips : 1 + 2 * chips])
        (by_source, total_in, col_taps, row_taps, out, held, image, padded, stage, result, sems,
         out_sems) = refs[1 + 2 * chips:]
        here = lax.axis_index("patch")
        core, chip = lax.rem(here, CORES), lax.div(here, CORES)
        left_over = words[0, 3]
        for p in range(1, places):
            left_over = left_over + words[p, 3]
        image[...] = total_in[...]

        @pl.when(left_over == 0)
        def _():
            for n in range(CORES):
                for d in range(chips):
                    sender = lax.rem(core + n, CORES)
                    p = lax.rem(chip - d + chips, chips) * CORES + sender
                    label = words[p, 2]

                    @pl.when(words[p, 1] == core)
                    def _(block=by_core[n][d], label=label):
                        spot = spot_of(label, edge, wide)
                        image[spot] = image[spot] + block[...].astype(F32)

        @pl.when(left_over > 0)
        def _():
            def begin(p, carry):
                @pl.when(words[p, 4] >= 0)
                def _():
                    pltpu.make_async_copy(by_source.at[p], held.at[p], sems.at[p]).start()

                return carry

            def add(p, carry):
                @pl.when(words[p, 4] >= 0)
                def _():
                    pltpu.make_async_copy(by_source.at[p], held.at[p], sems.at[p]).wait()
                    spot = spot_of(words[p, 4], edge, wide)
                    image[spot] = image[spot] + held[p].astype(F32)

                return carry

            lax.fori_loop(0, places, begin, 0)
            lax.fori_loop(0, places, add, 0)

        for r in range(0, height, LANE):
            padded[pl.ds(r, LANE), :] = shifted(image[pl.ds(r, LANE), :])
        copies = []
        for j in range(breadth // WINDOW):
            store_strip(result, filter_strip(padded, col_taps, row_taps, stage, j), j)
            spot = (pl.ds(0, height), pl.ds(j * WINDOW, WINDOW))
            copies.append(pltpu.make_async_copy(result.at[spot], out.at[spot], out_sems.at[j]))
            copies[-1].start()
        for copy in copies:
            copy.wait()

    return pl.pallas_call(
        kernel,
        out_shape=jax.ShapeDtypeStruct((height, breadth), F32),
        in_specs=[SMEM] + [VMEM] * (2 * chips) + [HBM] + [VMEM] * 3,
        out_specs=HBM,
        scratch_shapes=[
            pltpu.VMEM((places, edge, edge), BF16),
            pltpu.VMEM((height, breadth), F32),
            pltpu.VMEM((height, breadth + 2 * HALO), BF16),
            pltpu.VMEM((2, components * WINDOW, WINDOW), BF16),
            pltpu.VMEM((height, breadth), F32),
            pltpu.SemaphoreType.DMA((places,)),
            pltpu.SemaphoreType.DMA((breadth // WINDOW,)),
        ],
        compiler_params=PARAMS,
        name="finish",
    )(notes, *own, *other, second, total, col_table, row_table)


def per_device(
    blocks,
    block_patch,
    block_slot,
    block_count,
    template,
    basis_rows,
    basis_cols,
    coeffs,
    psf_rows,
    psf_cols,
):
    n_patch, n_visit = lax.axis_size("patch"), lax.axis_size("visit")
    chips = n_patch // CORES
    side = 4
    assert side * side == n_visit
    pieces, patches = blocks[0, 0], block_patch.reshape(-1)
    slots, count = block_slot.reshape(-1), block_count.reshape(-1)

    def to_chip(d):
        return [(i, (i + CORES * d) % n_patch) for i in range(n_patch)]

    outgoing = pack_main(pieces, patches, slots, count, n_patch)
    arrived = lax.all_to_all(outgoing, "patch", 0, 0, tiled=True)

    def along_x(d):
        return [(i, i // side * side + (i + d) % side) for i in range(n_visit)]

    def along_y(d):
        return [(i, (i + side * d) % n_visit) for i in range(n_visit)]

    rows = template[0]
    near = [rows] + [lax.ppermute(rows, "visit", along_x(d)) for d in range(1, side)]
    near = jnp.concatenate(near, axis=0)
    groups = [near] + [lax.ppermute(near, "visit", along_y(d)) for d in range(1, side)]
    scaled = coeffs[0][:, None] * basis_cols
    me = lax.axis_index("visit").reshape(1).astype(jnp.int32)
    model, col_table, row_table = make_model(
        groups, me, basis_rows.astype(F32), scaled, psf_rows[0].astype(F32),
        psf_cols[0].astype(F32),
    )
    extra = pack_extra(pieces, patches, count, col_table, n_patch)
    neighbour = [(i, i ^ 1) for i in range(n_patch)]
    own, other = list(extra), [None] * chips
    for d in sorted(range(chips), key=lambda d: min(d, chips - d)):
        if d:
            own[d] = lax.ppermute(extra[d], "patch", to_chip(d))
        other[d] = lax.ppermute(own[d], "patch", neighbour)
    edge = pieces.shape[1]
    notes = arrived[:, edge, :NOTE_WORDS].astype(jnp.int32)
    total = add_first(notes, arrived, model)

    def by_source():
        second = pack_second(pieces, patches, count, n_patch)
        return lax.all_to_all(second, "patch", 0, 0, tiled=True)

    def by_chip():
        return no_second((n_patch, edge, edge), pieces.dtype)

    second = lax.cond(jnp.any(notes[:, 3] > 0), by_source, by_chip)
    filtered = finish(notes, own, other, second, total, col_table, row_table)
    return filtered[None, None]


def solution(mesh):
    placed = (
        P("patch", "visit", None, None, None),
        P("patch", "visit", None, None),
        P("patch", "visit", None),
        P("patch", "visit"),
        P("patch", "visit", None),
        P(),
        P(),
        P("visit", None),
        P("visit", None, None),
        P("visit", None, None),
    )
    return jax.shard_map(
        per_device,
        mesh=mesh,
        in_specs=placed,
        out_specs=P("patch", "visit", None, None),
        check_vma=False,
    )
```

```python
import jax
import jax.numpy as jnp
from jax import lax
from jax.experimental import pallas as pl
from jax.experimental.pallas import tpu as pltpu
from jax.sharding import PartitionSpec as P

CORES = 2
NOTE_ROWS = 16
LANE = 128
HALO = 64
WINDOW = 256
LAP = 16
F32 = jnp.float32
BF16 = jnp.bfloat16
PARAMS = pltpu.CompilerParams(vmem_limit_bytes=48 * 1024 * 1024)
SMEM = pl.BlockSpec(memory_space=pltpu.SMEM)
VMEM = pl.BlockSpec(memory_space=pltpu.VMEM)
ANY = pl.BlockSpec(memory_space=pl.ANY)


def scan_entries(lists, first, extra, late, chips, here):
    patch, count, entries = lists
    for q in range(first.shape[0]):
        first[q] = -1
        late[q] = -1
    for d in range(chips):
        extra[d] = -1

    def visit(i, left_over):
        q = patch[i]
        again = first[q] >= 0
        d = lax.rem(lax.div(q, CORES) - here + chips, chips)
        taken = extra[d] >= 0

        @pl.when(jnp.logical_not(again))
        def _():
            first[q] = i

        @pl.when(jnp.logical_and(again, jnp.logical_not(taken)))
        def _():
            extra[d] = i

        @pl.when(jnp.logical_and(again, taken))
        def _():
            late[q] = i

        return left_over + jnp.logical_and(again, taken).astype(jnp.int32)

    return lax.fori_loop(0, jnp.minimum(count[0], entries), visit, jnp.int32(0))


def copy_entry(blocks, i, target, start, edge):
    @pl.when(i >= 0)
    def _():
        target[pl.ds(start, edge), :] = blocks[jnp.maximum(i, 0)]


def note_rows(words, edge, dtype):
    lane = lax.broadcasted_iota(jnp.int32, (NOTE_ROWS, edge), 1)
    row = jnp.zeros((NOTE_ROWS, edge), jnp.int32)
    for n, word in enumerate(words):
        row = jnp.where(lane == n, word, row)
    return row.astype(F32).astype(dtype)


def slot_of(slot, i):
    return jnp.where(i >= 0, slot[jnp.maximum(i, 0)], -1)


def pack_kernel(patch, slot, count, blocks, rows, *refs):
    outs = refs[:-4]
    refs[-4][...] = rows[...]
    first, extra, late = refs[-3:]
    chips, edge = len(outs), blocks.shape[1]
    here = lax.div(lax.axis_index("patch"), CORES)
    left_over = scan_entries((patch, count, blocks.shape[0]), first, extra, late, chips, here)
    for d, out in enumerate(outs):
        chip = lax.rem(here + d, chips)
        mains = [first[chip * CORES + c] for c in range(CORES)]
        e = extra[d]
        for n, i in enumerate(mains + [e]):
            copy_entry(blocks, i, out, n * edge, edge)
        words = [slot_of(slot, i) for i in mains]
        words += [
            jnp.where(e >= 0, lax.rem(patch[jnp.maximum(e, 0)], CORES), -1),
            slot_of(slot, e),
            left_over,
        ]
        out[pl.ds((CORES + 1) * edge, NOTE_ROWS), :] = note_rows(words, edge, out.dtype)


def list_scratch(places):
    return [
        pltpu.SMEM((places,), jnp.int32),
        pltpu.SMEM((places // CORES,), jnp.int32),
        pltpu.SMEM((places,), jnp.int32),
    ]


def pack(blocks, block_patch, block_slot, block_count, template, places):
    edge = blocks.shape[1]
    rows = (CORES + 1) * edge + NOTE_ROWS
    chips = places // CORES
    return pl.pallas_call(
        pack_kernel,
        out_shape=(jax.ShapeDtypeStruct((rows, edge), blocks.dtype),) * chips
        + (jax.ShapeDtypeStruct(template.shape, template.dtype),),
        in_specs=[SMEM, SMEM, SMEM, VMEM, VMEM],
        out_specs=(VMEM,) * (chips + 1),
        scratch_shapes=list_scratch(places),
        compiler_params=PARAMS,
        name="pack",
    )(block_patch, block_slot, block_count, blocks, template)


def pack_late_kernel(patch, slot, count, blocks, out, first, extra, late):
    places, edge = out.shape[0], blocks.shape[1]
    here = lax.div(lax.axis_index("patch"), CORES)
    scan_entries((patch, count, blocks.shape[0]), first, extra, late, places // CORES, here)
    for q in range(places):
        copy_entry(blocks, late[q], out.at[q], 0, edge)
        out[q, pl.ds(edge, NOTE_ROWS), :] = note_rows([slot_of(slot, late[q])], edge, out.dtype)


def pack_late(blocks, block_patch, block_slot, block_count, places):
    edge = blocks.shape[1]
    return pl.pallas_call(
        pack_late_kernel,
        out_shape=jax.ShapeDtypeStruct((places, edge + NOTE_ROWS, edge), blocks.dtype),
        in_specs=[SMEM, SMEM, SMEM, VMEM],
        out_specs=VMEM,
        scratch_shapes=list_scratch(places),
        compiler_params=PARAMS,
        name="pack_late",
    )(block_patch, block_slot, block_count, blocks)


def fill_band(table, taps, index, row0, col0, height, breadth, sign, base):
    length = taps.shape[1]
    for r in range(0, height, 16):
        rows = lax.broadcasted_iota(jnp.int32, (16, breadth), 0)
        cols = lax.broadcasted_iota(jnp.int32, (16, breadth), 1)
        offset = sign * (rows - cols) + (sign * r + base)
        values = jnp.zeros((16, breadth), F32)
        for u in range(length):
            values = jnp.where(offset == u, taps[index, u], values)
        table[pl.ds(row0 + r, 16), pl.ds(col0, breadth)] = values.astype(table.dtype)


def fill_tables(col_table, row_table, col_taps, row_taps):
    half = col_taps.shape[1] // 2
    for k in range(col_taps.shape[0]):
        fill_band(col_table, col_taps, k, 0, k * LANE, WINDOW, LANE, 1, half - HALO)
        for w in range(2):
            fill_band(
                row_table.at[w], row_taps, k, 0, k * WINDOW, WINDOW + LAP, WINDOW, -1,
                half + w * LAP,
            )


def shifted(values):
    rows = values.shape[0]
    edge = jnp.zeros((rows, HALO), F32)
    return jnp.concatenate([edge, values, edge], axis=1).astype(BF16)


def filter_strip(padded, col_table, row_table, stage, strip):
    count = col_table.shape[1] // LANE
    for h in range(2):
        start = strip * WINDOW + h * LANE
        if not isinstance(start, int):
            start = pl.multiple_of(start, LANE)
        for w in range(2):
            across = jnp.dot(
                padded[pl.ds(w * WINDOW, WINDOW), pl.ds(start, WINDOW)],
                col_table[...],
                preferred_element_type=F32,
            ).astype(BF16)
            for k in range(count):
                stage[w, pl.ds(k * WINDOW, WINDOW), pl.ds(h * LANE, LANE)] = across[
                    :, k * LANE : (k + 1) * LANE
                ]
    top = jnp.dot(row_table[0], stage[0], preferred_element_type=F32)
    low = jnp.dot(row_table[1], stage[1], preferred_element_type=F32)
    cut = WINDOW - LAP
    return top[:cut], top[cut:] + low[: 2 * LAP], low[2 * LAP :]


def store_strip(target, parts, strip):
    start = strip * WINDOW
    if not isinstance(start, int):
        start = pl.multiple_of(start, LANE)
    row = 0
    for part in parts:
        target[pl.ds(row, part.shape[0]), pl.ds(start, WINDOW)] = part
        row += part.shape[0]


def make_model(gathered, basis_rows, scaled, psf_rows, psf_cols):
    parts, local_rows, breadth = gathered.shape
    height = parts * local_rows
    basis, components = basis_rows.shape[0], psf_rows.shape[0]

    def kernel(source, basis_taps, scaled_taps, psf_row_taps, psf_col_taps, less, psf_col_table,
               psf_row_table, padded, col_table, row_table, stage):
        fill_tables(col_table, row_table, basis_taps, scaled_taps)
        for v in range(parts):
            padded[pl.ds(v * local_rows, local_rows), :] = shifted(source[v].astype(F32))

        def strip(j, carry):
            parts = filter_strip(padded, col_table, row_table, stage, j)
            store_strip(less, [-part for part in parts], j)
            return carry

        lax.fori_loop(0, breadth // WINDOW, strip, 0)
        fill_tables(psf_col_table, psf_row_table, psf_row_taps, psf_col_taps)

    return pl.pallas_call(
        kernel,
        out_shape=(
            jax.ShapeDtypeStruct((height, breadth), F32),
            jax.ShapeDtypeStruct((WINDOW, components * LANE), BF16),
            jax.ShapeDtypeStruct((2, WINDOW + LAP, components * WINDOW), BF16),
        ),
        in_specs=[VMEM] + [SMEM] * 4,
        out_specs=(VMEM, VMEM, VMEM),
        scratch_shapes=[
            pltpu.VMEM((height, breadth + 2 * HALO), BF16),
            pltpu.VMEM((WINDOW, basis * LANE), BF16),
            pltpu.VMEM((2, WINDOW + LAP, basis * WINDOW), BF16),
            pltpu.VMEM((2, basis * WINDOW, WINDOW), BF16),
        ],
        compiler_params=PARAMS,
        name="model",
    )(gathered, basis_rows, scaled, psf_rows, psf_cols)


def add_block(image, label, block):
    edge = block.shape[0]
    wide = image.shape[1] // edge

    @pl.when(label >= 0)
    def _():
        row = pl.multiple_of(lax.div(label, wide) * edge, edge)
        col = pl.multiple_of(lax.rem(label, wide) * edge, edge)
        spot = (pl.ds(row, edge), pl.ds(col, edge))
        image[spot] = image[spot] + block[...].astype(F32)


def read_notes(notes, lines, words, sem):
    for g, note in enumerate(notes):
        lines[pl.ds(g, 1), :] = note[:, :LANE].astype(F32).astype(jnp.int32)[:1]
    copy = pltpu.make_async_copy(lines, words, sem)
    copy.start()
    copy.wait()


def note_scratch(number):
    lines = -(-number // 8) * 8
    return [
        pltpu.VMEM((lines, LANE), jnp.int32),
        pltpu.SMEM((lines, LANE), jnp.int32),
        pltpu.SemaphoreType.DMA,
    ]


def take_blocks(image, sources, lines, words, sem):
    rows, edge = sources[0].shape
    core = lax.rem(lax.axis_index("patch"), CORES)
    read_notes([x[pl.ds(rows - NOTE_ROWS, NOTE_ROWS), :] for x in sources], lines, words, sem)
    count = jnp.int32(0)
    for g, source in enumerate(sources):
        count = count + words[g, 4]
        mine = pl.multiple_of(core * edge, edge)
        add_block(image, words[g, core], source.at[pl.ds(mine, edge)])
        extra = jnp.where(words[g, 2] == core, words[g, 3], -1)
        add_block(image, extra, source.at[pl.ds(CORES * edge, edge)])
    return count


def take(total, arrays):
    number = len(arrays)

    def kernel(*refs):
        image, left_over, lines, words, sem = refs[1 + number:]
        image[...] = refs[0][...]
        left_over[0] = take_blocks(image, refs[1 : 1 + number], lines, words, sem)

    return pl.pallas_call(
        kernel,
        out_shape=(
            jax.ShapeDtypeStruct(total.shape, total.dtype),
            jax.ShapeDtypeStruct((1,), jnp.int32),
        ),
        in_specs=[VMEM] * (1 + number),
        out_specs=(VMEM, SMEM),
        scratch_shapes=note_scratch(number),
        input_output_aliases={0: 0},
        compiler_params=PARAMS,
        name="take",
    )(total, *arrays)


def finish(total, arrays, before, col_table, row_table, late=None):
    height, breadth = total.shape
    components = col_table.shape[1] // LANE
    number, edge = len(arrays), arrays[0].shape[1]
    lates = [] if late is None else [late]
    places = late.shape[0] if lates else 0

    def kernel(*refs):
        total_in, before_in, col_taps, row_taps = refs[:4]
        sources = refs[4 : 4 + number]
        late_blocks = refs[4 + number : 4 + number + len(lates)]
        (out, left_over, image, padded, stage, result, out_sems, lines, words,
         sem) = refs[4 + number + len(lates):]
        image[...] = total_in[...]
        left_over[0] = before_in[0] + take_blocks(image, sources, lines, words, sem)
        for blocks in late_blocks:
            read_notes(
                [blocks[p, pl.ds(edge, NOTE_ROWS), :] for p in range(places)], lines, words, sem
            )
            for p in range(places):
                add_block(image, words[p, 0], blocks.at[p, pl.ds(0, edge)])
        for r in range(0, height, LANE):
            padded[pl.ds(r, LANE), :] = shifted(image[pl.ds(r, LANE), :])
        copies = []
        for j in range(breadth // WINDOW):
            store_strip(result, filter_strip(padded, col_taps, row_taps, stage, j), j)
            spot = (pl.ds(0, height), pl.ds(j * WINDOW, WINDOW))
            copies.append(pltpu.make_async_copy(result.at[spot], out.at[spot], out_sems.at[j]))
            copies[-1].start()
        for copy in copies:
            copy.wait()

    return pl.pallas_call(
        kernel,
        out_shape=(
            jax.ShapeDtypeStruct((height, breadth), F32),
            jax.ShapeDtypeStruct((1,), jnp.int32),
        ),
        in_specs=[VMEM, SMEM] + [VMEM] * (2 + number + len(lates)),
        out_specs=(ANY, SMEM),
        scratch_shapes=[
            pltpu.VMEM((height, breadth), F32),
            pltpu.VMEM((height, breadth + 2 * HALO), BF16),
            pltpu.VMEM((2, components * WINDOW, WINDOW), BF16),
            pltpu.VMEM((height, breadth), F32),
            pltpu.SemaphoreType.DMA((breadth // WINDOW,)),
        ] + note_scratch(max(number, places)),
        compiler_params=PARAMS,
        name="finish_late" if lates else "finish",
    )(total, before, col_table, row_table, *arrays, *lates)


def per_device(
    blocks,
    block_patch,
    block_slot,
    block_count,
    template,
    basis_rows,
    basis_cols,
    coeffs,
    psf_rows,
    psf_cols,
):
    n_patch, n_visit = lax.axis_size("patch"), lax.axis_size("visit")
    chips = n_patch // CORES
    pieces, patches = blocks[0, 0], block_patch.reshape(-1)
    slots, count = block_slot.reshape(-1), block_count.reshape(-1)

    def to_chip(d):
        return [(i, (i + CORES * d) % n_patch) for i in range(n_patch)]

    *came, rows = pack(pieces, patches, slots, count, template[0], n_patch)
    near_last = sorted(range(1, chips), key=lambda d: -min(d, chips - d))
    early, last = near_last[:-2], near_last[-2:]
    for d in early:
        came[d] = lax.ppermute(came[d], "patch", to_chip(d))

    spread = jnp.broadcast_to(rows[None], (n_visit, *rows.shape))
    gathered = lax.all_to_all(spread, "visit", 0, 0, tiled=True)
    scaled = coeffs[0][:, None] * basis_cols
    total, col_table, row_table = make_model(
        gathered, basis_rows.astype(F32), scaled, psf_rows[0].astype(F32),
        psf_cols[0].astype(F32),
    )
    neighbour = [(i, i ^ 1) for i in range(n_patch)]
    for d in last:
        came[d], _ = lax.optimization_barrier((came[d], col_table))
        came[d] = lax.ppermute(came[d], "patch", to_chip(d))
    other = [None] * chips
    for d in [0] + early + last:
        came[d], _ = lax.optimization_barrier((came[d], col_table))
        other[d] = lax.ppermute(came[d], "patch", neighbour)
    total, before = take(total, [came[d] for d in [0] + early] + [other[d] for d in [0] + early])
    final = [came[d] for d in last] + [other[d] for d in last]
    filtered, left_over = finish(total, final, before, col_table, row_table)

    def send_late(carry):
        late = pack_late(pieces, patches, slots, count, n_patch)
        late = lax.all_to_all(late, "patch", 0, 0, tiled=True)
        image, _ = finish(total, final, before, col_table, row_table, late)
        return jnp.zeros_like(carry[0]), image

    filtered = lax.while_loop(lambda carry: carry[0][0] > 0, send_late, (left_over, filtered))[1]
    return filtered[None, None]


def solution(mesh):
    placed = (
        P("patch", "visit", None, None, None),
        P("patch", "visit", None, None),
        P("patch", "visit", None),
        P("patch", "visit"),
        P("patch", "visit", None),
        P(),
        P(),
        P("visit", None),
        P("visit", None, None),
        P("visit", None, None),
    )
    return jax.shard_map(
        per_device,
        mesh=mesh,
        in_specs=placed,
        out_specs=P("patch", "visit", None, None),
        check_vma=False,
    )
```

```python
import jax
import jax.numpy as jnp
from jax import lax
from jax.experimental import pallas as pl
from jax.experimental.pallas import tpu as pltpu
from jax.sharding import PartitionSpec as P

CORES = 2
NOTE_ROWS = 16
NOTE_WORDS = 8
LANE = 128
HALO = 64
WINDOW = 256
LAP = 16
F32 = jnp.float32
BF16 = jnp.bfloat16
PARAMS = pltpu.CompilerParams(vmem_limit_bytes=48 * 1024 * 1024)
SMEM = pl.BlockSpec(memory_space=pltpu.SMEM)
VMEM = pl.BlockSpec(memory_space=pltpu.VMEM)
HBM = pl.BlockSpec(memory_space=pltpu.HBM)


def scan_entries(lists, first, second, extra, chips, here):
    patch, count, entries = lists
    for q in range(first.shape[0]):
        first[q] = -1
        second[q] = -1
    for d in range(chips):
        extra[d] = -1

    def visit(i, left_over):
        q = patch[i]
        again = first[q] >= 0
        d = lax.rem(lax.div(q, CORES) - here + chips, chips)
        taken = extra[d] >= 0

        @pl.when(jnp.logical_not(again))
        def _():
            first[q] = i

        @pl.when(again)
        def _():
            second[q] = i

        @pl.when(jnp.logical_and(again, jnp.logical_not(taken)))
        def _():
            extra[d] = i

        return left_over + jnp.logical_and(again, taken).astype(jnp.int32)

    return lax.fori_loop(0, jnp.minimum(count[0], entries), visit, jnp.int32(0))


def copy_entry(blocks, i, target):
    @pl.when(i >= 0)
    def _():
        target[...] = blocks[jnp.maximum(i, 0)]


def list_scratch(places):
    return [
        pltpu.SMEM((places,), jnp.int32),
        pltpu.SMEM((places,), jnp.int32),
        pltpu.SMEM((places // CORES,), jnp.int32),
    ]


def pack_extra_kernel(patch, count, blocks, after, *refs):
    chips = len(refs) - 3
    outs = refs[:chips]
    first, second, extra = refs[chips:]
    here = lax.div(lax.axis_index("patch"), CORES)
    scan_entries((patch, count, blocks.shape[0]), first, second, extra, chips, here)
    for d in range(chips):
        copy_entry(blocks, extra[d], outs[d])


def pack_extra(blocks, block_patch, block_count, after, places):
    edge = blocks.shape[1]
    chips = places // CORES
    return pl.pallas_call(
        pack_extra_kernel,
        out_shape=(jax.ShapeDtypeStruct((edge, edge), blocks.dtype),) * chips,
        in_specs=[SMEM, SMEM, VMEM, VMEM],
        out_specs=(VMEM,) * chips,
        scratch_shapes=list_scratch(places),
        compiler_params=PARAMS,
        name="pack_extra",
    )(block_patch, block_count, blocks, after)


def pack_main_kernel(patch, slot, count, blocks, outgoing, first, second, extra):
    places = outgoing.shape[0]
    edge = blocks.shape[1]
    chips = places // CORES
    here = lax.div(lax.axis_index("patch"), CORES)
    left_over = scan_entries((patch, count, blocks.shape[0]), first, second, extra, chips, here)
    lane = lax.broadcasted_iota(jnp.int32, (NOTE_ROWS, edge), 1)
    for q in range(places):
        i, j = first[q], second[q]
        e = extra[lax.rem(q // CORES - here + chips, chips)]
        copy_entry(blocks, i, outgoing.at[q, pl.ds(0, edge)])
        words = (
            jnp.where(i >= 0, slot[jnp.maximum(i, 0)], -1),
            jnp.where(e >= 0, lax.rem(patch[jnp.maximum(e, 0)], CORES), -1),
            jnp.where(e >= 0, slot[jnp.maximum(e, 0)], -1),
            left_over,
            jnp.where(j >= 0, slot[jnp.maximum(j, 0)], -1),
        )
        row = jnp.zeros((NOTE_ROWS, edge), jnp.int32)
        for n, word in enumerate(words):
            row = jnp.where(lane == n, word, row)
        outgoing[q, pl.ds(edge, NOTE_ROWS), :] = row.astype(F32).astype(outgoing.dtype)


def pack_main(blocks, block_patch, block_slot, block_count, places):
    edge = blocks.shape[1]
    return pl.pallas_call(
        pack_main_kernel,
        out_shape=jax.ShapeDtypeStruct((places, edge + NOTE_ROWS, edge), blocks.dtype),
        in_specs=[SMEM, SMEM, SMEM, VMEM],
        out_specs=VMEM,
        scratch_shapes=list_scratch(places),
        compiler_params=PARAMS,
        name="pack_main",
    )(block_patch, block_slot, block_count, blocks)


def pack_second_kernel(patch, count, blocks, outgoing, first, second, extra):
    places = outgoing.shape[0]
    here = lax.div(lax.axis_index("patch"), CORES)
    scan_entries((patch, count, blocks.shape[0]), first, second, extra, places // CORES, here)
    for q in range(places):
        copy_entry(blocks, second[q], outgoing.at[q])


def pack_second(blocks, block_patch, block_count, places):
    edge = blocks.shape[1]
    return pl.pallas_call(
        pack_second_kernel,
        out_shape=jax.ShapeDtypeStruct((places, edge, edge), blocks.dtype),
        in_specs=[SMEM, SMEM, VMEM],
        out_specs=VMEM,
        scratch_shapes=list_scratch(places),
        compiler_params=PARAMS,
        name="pack_second",
    )(block_patch, block_count, blocks)


def fill_band(table, taps, index, row0, col0, height, breadth, sign, base):
    length = taps.shape[1]
    for r in range(0, height, 16):
        rows = lax.broadcasted_iota(jnp.int32, (16, breadth), 0)
        cols = lax.broadcasted_iota(jnp.int32, (16, breadth), 1)
        offset = sign * (rows - cols) + (sign * r + base)
        values = jnp.zeros((16, breadth), F32)
        for u in range(length):
            values = jnp.where(offset == u, taps[index, u], values)
        table[pl.ds(row0 + r, 16), pl.ds(col0, breadth)] = values.astype(table.dtype)


def fill_tables(col_table, row_table, col_taps, row_taps):
    half = col_taps.shape[1] // 2
    for k in range(col_taps.shape[0]):
        fill_band(col_table, col_taps, k, 0, k * LANE, WINDOW, LANE, 1, half - HALO)
        for w in range(2):
            fill_band(
                row_table.at[w], row_taps, k, 0, k * WINDOW, WINDOW + LAP, WINDOW, -1,
                half + w * LAP,
            )


def shifted(values):
    rows = values.shape[0]
    edge = jnp.zeros((rows, HALO), F32)
    return jnp.concatenate([edge, values, edge], axis=1).astype(BF16)


def filter_strip(padded, col_table, row_table, stage, strip):
    count = col_table.shape[1] // LANE
    for h in range(2):
        start = strip * WINDOW + h * LANE
        if not isinstance(start, int):
            start = pl.multiple_of(start, LANE)
        for w in range(2):
            across = jnp.dot(
                padded[pl.ds(w * WINDOW, WINDOW), pl.ds(start, WINDOW)],
                col_table[...],
                preferred_element_type=F32,
            ).astype(BF16)
            for k in range(count):
                stage[w, pl.ds(k * WINDOW, WINDOW), pl.ds(h * LANE, LANE)] = across[
                    :, k * LANE : (k + 1) * LANE
                ]
    top = jnp.dot(row_table[0], stage[0], preferred_element_type=F32)
    low = jnp.dot(row_table[1], stage[1], preferred_element_type=F32)
    cut = WINDOW - LAP
    return top[:cut], top[cut:] + low[: 2 * LAP], low[2 * LAP :]


def store_strip(target, parts, strip):
    start = strip * WINDOW
    if not isinstance(start, int):
        start = pl.multiple_of(start, LANE)
    row = 0
    for part in parts:
        target[pl.ds(row, part.shape[0]), pl.ds(start, WINDOW)] = part
        row += part.shape[0]


def make_model(pieces, me, basis_rows, scaled, psf_rows, psf_cols):
    parts = len(pieces)
    group_rows, breadth = pieces[0].shape
    local_rows = group_rows // parts
    height = parts * group_rows
    basis, components = basis_rows.shape[0], psf_rows.shape[0]

    def kernel(*refs):
        sources = refs[:parts]
        (position, basis_taps, scaled_taps, psf_row_taps, psf_col_taps, less, psf_col_table,
         psf_row_table, padded, col_table, row_table, stage) = refs[parts:]
        fill_tables(col_table, row_table, basis_taps, scaled_taps)
        y, x = lax.div(position[0], parts), lax.rem(position[0], parts)
        for dy, source in enumerate(sources):
            for dx in range(parts):
                owner = lax.rem(y - dy + parts, parts) * parts + lax.rem(x - dx + parts, parts)
                start = pl.multiple_of(owner * local_rows, local_rows)
                padded[pl.ds(start, local_rows), :] = shifted(
                    source[pl.ds(dx * local_rows, local_rows), :].astype(F32)
                )

        def strip(j, carry):
            parts = filter_strip(padded, col_table, row_table, stage, j)
            store_strip(less, [-part for part in parts], j)
            return carry

        lax.fori_loop(0, breadth // WINDOW, strip, 0)
        fill_tables(psf_col_table, psf_row_table, psf_row_taps, psf_col_taps)

    return pl.pallas_call(
        kernel,
        out_shape=(
            jax.ShapeDtypeStruct((height, breadth), F32),
            jax.ShapeDtypeStruct((WINDOW, components * LANE), BF16),
            jax.ShapeDtypeStruct((2, WINDOW + LAP, components * WINDOW), BF16),
        ),
        in_specs=[VMEM] * parts + [SMEM] * 5,
        out_specs=(VMEM, VMEM, VMEM),
        scratch_shapes=[
            pltpu.VMEM((height, breadth + 2 * HALO), BF16),
            pltpu.VMEM((WINDOW, basis * LANE), BF16),
            pltpu.VMEM((2, WINDOW + LAP, basis * WINDOW), BF16),
            pltpu.VMEM((2, basis * WINDOW, WINDOW), BF16),
        ],
        compiler_params=PARAMS,
        name="model",
    )(*pieces, me, basis_rows, scaled, psf_rows, psf_cols)


def spot_of(label, edge, wide):
    row = pl.multiple_of(lax.div(label, wide) * edge, edge)
    col = pl.multiple_of(lax.rem(label, wide) * edge, edge)
    return pl.ds(row, edge), pl.ds(col, edge)


def add_first(notes, main, model_negative):
    height, breadth = model_negative.shape
    places, edge = main.shape[0], main.shape[2]

    def kernel(words, blocks, less, total):
        total[...] = less[...]

        def step(p, carry):
            label = words[p, 0]

            @pl.when(label >= 0)
            def _():
                spot = spot_of(label, edge, breadth // edge)
                total[spot] = total[spot] + blocks[p, pl.ds(0, edge), :].astype(F32)

            return carry

        lax.fori_loop(0, places, step, 0)

    return pl.pallas_call(
        kernel,
        out_shape=jax.ShapeDtypeStruct((height, breadth), F32),
        in_specs=[SMEM, VMEM, VMEM],
        out_specs=VMEM,
        compiler_params=PARAMS,
        name="add_first",
    )(notes, main, model_negative)


def no_second(shape, dtype):
    return pl.pallas_call(
        lambda out: None,
        out_shape=jax.ShapeDtypeStruct(shape, dtype),
        out_specs=HBM,
        compiler_params=PARAMS,
        name="no_second",
    )()


def finish(notes, own, other, second, total, col_table, row_table):
    height, breadth = total.shape
    places, edge = notes.shape[0], second.shape[1]
    components = col_table.shape[1] // LANE
    chips = len(own)
    wide = breadth // edge

    def kernel(*refs):
        words, by_core = refs[0], (refs[1 : 1 + chips], refs[1 + chips : 1 + 2 * chips])
        (by_source, total_in, col_taps, row_taps, out, held, image, padded, stage, result, sems,
         out_sems) = refs[1 + 2 * chips:]
        here = lax.axis_index("patch")
        core, chip = lax.rem(here, CORES), lax.div(here, CORES)
        left_over = words[0, 3]
        for p in range(1, places):
            left_over = left_over + words[p, 3]
        image[...] = total_in[...]

        @pl.when(left_over == 0)
        def _():
            for n in range(CORES):
                for d in range(chips):
                    sender = lax.rem(core + n, CORES)
                    p = lax.rem(chip - d + chips, chips) * CORES + sender
                    label = words[p, 2]

                    @pl.when(words[p, 1] == core)
                    def _(block=by_core[n][d], label=label):
                        spot = spot_of(label, edge, wide)
                        image[spot] = image[spot] + block[...].astype(F32)

        @pl.when(left_over > 0)
        def _():
            def begin(p, carry):
                @pl.when(words[p, 4] >= 0)
                def _():
                    pltpu.make_async_copy(by_source.at[p], held.at[p], sems.at[p]).start()

                return carry

            def add(p, carry):
                @pl.when(words[p, 4] >= 0)
                def _():
                    pltpu.make_async_copy(by_source.at[p], held.at[p], sems.at[p]).wait()
                    spot = spot_of(words[p, 4], edge, wide)
                    image[spot] = image[spot] + held[p].astype(F32)

                return carry

            lax.fori_loop(0, places, begin, 0)
            lax.fori_loop(0, places, add, 0)

        for r in range(0, height, LANE):
            padded[pl.ds(r, LANE), :] = shifted(image[pl.ds(r, LANE), :])
        copies = []
        for j in range(breadth // WINDOW):
            store_strip(result, filter_strip(padded, col_taps, row_taps, stage, j), j)
            spot = (pl.ds(0, height), pl.ds(j * WINDOW, WINDOW))
            copies.append(pltpu.make_async_copy(result.at[spot], out.at[spot], out_sems.at[j]))
            copies[-1].start()
        for copy in copies:
            copy.wait()

    return pl.pallas_call(
        kernel,
        out_shape=jax.ShapeDtypeStruct((height, breadth), F32),
        in_specs=[SMEM] + [VMEM] * (2 * chips) + [HBM] + [VMEM] * 3,
        out_specs=HBM,
        scratch_shapes=[
            pltpu.VMEM((places, edge, edge), BF16),
            pltpu.VMEM((height, breadth), F32),
            pltpu.VMEM((height, breadth + 2 * HALO), BF16),
            pltpu.VMEM((2, components * WINDOW, WINDOW), BF16),
            pltpu.VMEM((height, breadth), F32),
            pltpu.SemaphoreType.DMA((places,)),
            pltpu.SemaphoreType.DMA((breadth // WINDOW,)),
        ],
        compiler_params=PARAMS,
        name="finish",
    )(notes, *own, *other, second, total, col_table, row_table)


def per_device(
    blocks,
    block_patch,
    block_slot,
    block_count,
    template,
    basis_rows,
    basis_cols,
    coeffs,
    psf_rows,
    psf_cols,
):
    n_patch, n_visit = lax.axis_size("patch"), lax.axis_size("visit")
    chips = n_patch // CORES
    side = 4
    assert side * side == n_visit
    pieces, patches = blocks[0, 0], block_patch.reshape(-1)
    slots, count = block_slot.reshape(-1), block_count.reshape(-1)

    def to_chip(d):
        return [(i, (i + CORES * d) % n_patch) for i in range(n_patch)]

    outgoing = pack_main(pieces, patches, slots, count, n_patch)
    arrived = lax.all_to_all(outgoing, "patch", 0, 0, tiled=True)

    def along_x(d):
        return [(i, i // side * side + (i + d) % side) for i in range(n_visit)]

    def along_y(d):
        return [(i, (i + side * d) % n_visit) for i in range(n_visit)]

    rows = template[0]
    near = [rows] + [lax.ppermute(rows, "visit", along_x(d)) for d in range(1, side)]
    near = jnp.concatenate(near, axis=0)
    groups = [near] + [lax.ppermute(near, "visit", along_y(d)) for d in range(1, side)]
    scaled = coeffs[0][:, None] * basis_cols
    me = lax.axis_index("visit").reshape(1).astype(jnp.int32)
    total, col_table, row_table = make_model(
        groups, me, basis_rows.astype(F32), scaled, psf_rows[0].astype(F32),
        psf_cols[0].astype(F32),
    )
    extra = pack_extra(pieces, patches, count, col_table, n_patch)
    edge = pieces.shape[1]
    notes = arrived[:, edge, :NOTE_WORDS].astype(jnp.int32)
    total = add_first(notes, arrived, total)

    def by_source():
        second = pack_second(pieces, patches, count, n_patch)
        return lax.all_to_all(second, "patch", 0, 0, tiled=True)

    def by_chip():
        return no_second((n_patch, edge, edge), pieces.dtype)

    second = lax.cond(jnp.any(notes[:, 3] > 0), by_source, by_chip)
    neighbour = [(i, i ^ 1) for i in range(n_patch)]
    own, other = list(extra), [None] * chips
    near_last = sorted(range(1, chips), key=lambda d: -min(d, chips - d))
    for d in near_last:
        own[d] = lax.ppermute(extra[d], "patch", to_chip(d))
    for d in [0] + near_last:
        own[d], _ = lax.optimization_barrier((own[d], second))
        other[d] = lax.ppermute(own[d], "patch", neighbour)
    filtered = finish(notes, own, other, second, total, col_table, row_table)
    return filtered[None, None]


def solution(mesh):
    placed = (
        P("patch", "visit", None, None, None),
        P("patch", "visit", None, None),
        P("patch", "visit", None),
        P("patch", "visit"),
        P("patch", "visit", None),
        P(),
        P(),
        P("visit", None),
        P("visit", None, None),
        P("visit", None, None),
    )
    return jax.shard_map(
        per_device,
        mesh=mesh,
        in_specs=placed,
        out_specs=P("patch", "visit", None, None),
        check_vma=False,
    )
```

```python
import jax
import jax.numpy as jnp
from jax import lax
from jax.experimental import pallas as pl
from jax.experimental.pallas import tpu as pltpu
from jax.sharding import PartitionSpec as P

CORES = 2
NOTE_ROWS = 16
NOTE_WORDS = 8
LANE = 128
HALO = 64
WINDOW = 256
LAP = 16
F32 = jnp.float32
BF16 = jnp.bfloat16
PARAMS = pltpu.CompilerParams(vmem_limit_bytes=48 * 1024 * 1024)
SMEM = pl.BlockSpec(memory_space=pltpu.SMEM)
VMEM = pl.BlockSpec(memory_space=pltpu.VMEM)
HBM = pl.BlockSpec(memory_space=pltpu.HBM)


def scan_entries(lists, first, second, extra, chips, here):
    patch, count, entries = lists
    for q in range(first.shape[0]):
        first[q] = -1
        second[q] = -1
    for d in range(chips):
        extra[d] = -1

    def visit(i, left_over):
        q = patch[i]
        again = first[q] >= 0
        d = lax.rem(lax.div(q, CORES) - here + chips, chips)
        taken = extra[d] >= 0

        @pl.when(jnp.logical_not(again))
        def _():
            first[q] = i

        @pl.when(again)
        def _():
            second[q] = i

        @pl.when(jnp.logical_and(again, jnp.logical_not(taken)))
        def _():
            extra[d] = i

        return left_over + jnp.logical_and(again, taken).astype(jnp.int32)

    return lax.fori_loop(0, jnp.minimum(count[0], entries), visit, jnp.int32(0))


def copy_entry(blocks, i, target):
    @pl.when(i >= 0)
    def _():
        target[...] = blocks[jnp.maximum(i, 0)]


def list_scratch(places):
    return [
        pltpu.SMEM((places,), jnp.int32),
        pltpu.SMEM((places,), jnp.int32),
        pltpu.SMEM((places // CORES,), jnp.int32),
    ]


def pack_extra_kernel(patch, count, blocks, after, *refs):
    chips = len(refs) - 3
    outs = refs[:chips]
    first, second, extra = refs[chips:]
    here = lax.div(lax.axis_index("patch"), CORES)
    scan_entries((patch, count, blocks.shape[0]), first, second, extra, chips, here)
    for d in range(chips):
        copy_entry(blocks, extra[d], outs[d])


def pack_extra(blocks, block_patch, block_count, after, places):
    edge = blocks.shape[1]
    chips = places // CORES
    return pl.pallas_call(
        pack_extra_kernel,
        out_shape=(jax.ShapeDtypeStruct((edge, edge), blocks.dtype),) * chips,
        in_specs=[SMEM, SMEM, VMEM, VMEM],
        out_specs=(VMEM,) * chips,
        scratch_shapes=list_scratch(places),
        compiler_params=PARAMS,
        name="pack_extra",
    )(block_patch, block_count, blocks, after)


def pack_main_kernel(patch, slot, count, blocks, outgoing, first, second, extra):
    places = outgoing.shape[0]
    edge = blocks.shape[1]
    chips = places // CORES
    here = lax.div(lax.axis_index("patch"), CORES)
    left_over = scan_entries((patch, count, blocks.shape[0]), first, second, extra, chips, here)
    lane = lax.broadcasted_iota(jnp.int32, (NOTE_ROWS, edge), 1)
    for q in range(places):
        i, j = first[q], second[q]
        e = extra[lax.rem(q // CORES - here + chips, chips)]
        copy_entry(blocks, i, outgoing.at[q, pl.ds(0, edge)])
        words = (
            jnp.where(i >= 0, slot[jnp.maximum(i, 0)], -1),
            jnp.where(e >= 0, lax.rem(patch[jnp.maximum(e, 0)], CORES), -1),
            jnp.where(e >= 0, slot[jnp.maximum(e, 0)], -1),
            left_over,
            jnp.where(j >= 0, slot[jnp.maximum(j, 0)], -1),
        )
        row = jnp.zeros((NOTE_ROWS, edge), jnp.int32)
        for n, word in enumerate(words):
            row = jnp.where(lane == n, word, row)
        outgoing[q, pl.ds(edge, NOTE_ROWS), :] = row.astype(F32).astype(outgoing.dtype)


def pack_main(blocks, block_patch, block_slot, block_count, places):
    edge = blocks.shape[1]
    return pl.pallas_call(
        pack_main_kernel,
        out_shape=jax.ShapeDtypeStruct((places, edge + NOTE_ROWS, edge), blocks.dtype),
        in_specs=[SMEM, SMEM, SMEM, VMEM],
        out_specs=VMEM,
        scratch_shapes=list_scratch(places),
        compiler_params=PARAMS,
        name="pack_main",
    )(block_patch, block_slot, block_count, blocks)


def pack_second_kernel(patch, count, blocks, outgoing, first, second, extra):
    places = outgoing.shape[0]
    here = lax.div(lax.axis_index("patch"), CORES)
    scan_entries((patch, count, blocks.shape[0]), first, second, extra, places // CORES, here)
    for q in range(places):
        copy_entry(blocks, second[q], outgoing.at[q])


def pack_second(blocks, block_patch, block_count, places):
    edge = blocks.shape[1]
    return pl.pallas_call(
        pack_second_kernel,
        out_shape=jax.ShapeDtypeStruct((places, edge, edge), blocks.dtype),
        in_specs=[SMEM, SMEM, VMEM],
        out_specs=VMEM,
        scratch_shapes=list_scratch(places),
        compiler_params=PARAMS,
        name="pack_second",
    )(block_patch, block_count, blocks)


def fill_band(table, taps, index, row0, col0, height, breadth, sign, base):
    length = taps.shape[1]
    for r in range(0, height, 16):
        rows = lax.broadcasted_iota(jnp.int32, (16, breadth), 0)
        cols = lax.broadcasted_iota(jnp.int32, (16, breadth), 1)
        offset = sign * (rows - cols) + (sign * r + base)
        values = jnp.zeros((16, breadth), F32)
        for u in range(length):
            values = jnp.where(offset == u, taps[index, u], values)
        table[pl.ds(row0 + r, 16), pl.ds(col0, breadth)] = values.astype(table.dtype)


def fill_tables(col_table, row_table, col_taps, row_taps):
    half = col_taps.shape[1] // 2
    for k in range(col_taps.shape[0]):
        fill_band(col_table, col_taps, k, 0, k * LANE, WINDOW, LANE, 1, half - HALO)
        for w in range(2):
            fill_band(
                row_table.at[w], row_taps, k, 0, k * WINDOW, WINDOW + LAP, WINDOW, -1,
                half + w * LAP,
            )


def shifted(values):
    rows = values.shape[0]
    edge = jnp.zeros((rows, HALO), F32)
    return jnp.concatenate([edge, values, edge], axis=1).astype(BF16)


def filter_strip(padded, col_table, row_table, stage, strip):
    count = col_table.shape[1] // LANE
    for h in range(2):
        start = strip * WINDOW + h * LANE
        if not isinstance(start, int):
            start = pl.multiple_of(start, LANE)
        for w in range(2):
            across = jnp.dot(
                padded[pl.ds(w * WINDOW, WINDOW), pl.ds(start, WINDOW)],
                col_table[...],
                preferred_element_type=F32,
            ).astype(BF16)
            for k in range(count):
                stage[w, pl.ds(k * WINDOW, WINDOW), pl.ds(h * LANE, LANE)] = across[
                    :, k * LANE : (k + 1) * LANE
                ]
    top = jnp.dot(row_table[0], stage[0], preferred_element_type=F32)
    low = jnp.dot(row_table[1], stage[1], preferred_element_type=F32)
    cut = WINDOW - LAP
    return top[:cut], top[cut:] + low[: 2 * LAP], low[2 * LAP :]


def store_strip(target, parts, strip):
    start = strip * WINDOW
    if not isinstance(start, int):
        start = pl.multiple_of(start, LANE)
    row = 0
    for part in parts:
        target[pl.ds(row, part.shape[0]), pl.ds(start, WINDOW)] = part
        row += part.shape[0]


def make_model(pieces, me, basis_rows, scaled, psf_rows, psf_cols):
    parts = len(pieces)
    group_rows, breadth = pieces[0].shape
    local_rows = group_rows // parts
    height = parts * group_rows
    basis, components = basis_rows.shape[0], psf_rows.shape[0]

    def kernel(*refs):
        sources = refs[:parts]
        (position, basis_taps, scaled_taps, psf_row_taps, psf_col_taps, less, psf_col_table,
         psf_row_table, padded, col_table, row_table, stage) = refs[parts:]
        fill_tables(col_table, row_table, basis_taps, scaled_taps)
        y, x = lax.div(position[0], parts), lax.rem(position[0], parts)
        for dy, source in enumerate(sources):
            for dx in range(parts):
                owner = lax.rem(y - dy + parts, parts) * parts + lax.rem(x - dx + parts, parts)
                start = pl.multiple_of(owner * local_rows, local_rows)
                padded[pl.ds(start, local_rows), :] = shifted(
                    source[pl.ds(dx * local_rows, local_rows), :].astype(F32)
                )

        def strip(j, carry):
            parts = filter_strip(padded, col_table, row_table, stage, j)
            store_strip(less, [-part for part in parts], j)
            return carry

        lax.fori_loop(0, breadth // WINDOW, strip, 0)
        fill_tables(psf_col_table, psf_row_table, psf_row_taps, psf_col_taps)

    return pl.pallas_call(
        kernel,
        out_shape=(
            jax.ShapeDtypeStruct((height, breadth), F32),
            jax.ShapeDtypeStruct((WINDOW, components * LANE), BF16),
            jax.ShapeDtypeStruct((2, WINDOW + LAP, components * WINDOW), BF16),
        ),
        in_specs=[VMEM] * parts + [SMEM] * 5,
        out_specs=(VMEM, VMEM, VMEM),
        scratch_shapes=[
            pltpu.VMEM((height, breadth + 2 * HALO), BF16),
            pltpu.VMEM((WINDOW, basis * LANE), BF16),
            pltpu.VMEM((2, WINDOW + LAP, basis * WINDOW), BF16),
            pltpu.VMEM((2, basis * WINDOW, WINDOW), BF16),
        ],
        compiler_params=PARAMS,
        name="model",
    )(*pieces, me, basis_rows, scaled, psf_rows, psf_cols)


def spot_of(label, edge, wide):
    row = pl.multiple_of(lax.div(label, wide) * edge, edge)
    col = pl.multiple_of(lax.rem(label, wide) * edge, edge)
    return pl.ds(row, edge), pl.ds(col, edge)


def add_first(notes, main, model_negative):
    height, breadth = model_negative.shape
    places, edge = main.shape[0], main.shape[2]

    def kernel(words, blocks, less, total):
        total[...] = less[...]

        def step(p, carry):
            label = words[p, 0]

            @pl.when(label >= 0)
            def _():
                spot = spot_of(label, edge, breadth // edge)
                total[spot] = total[spot] + blocks[p, pl.ds(0, edge), :].astype(F32)

            return carry

        lax.fori_loop(0, places, step, 0)

    return pl.pallas_call(
        kernel,
        out_shape=jax.ShapeDtypeStruct((height, breadth), F32),
        in_specs=[SMEM, VMEM, VMEM],
        out_specs=VMEM,
        compiler_params=PARAMS,
        name="add_first",
    )(notes, main, model_negative)


def no_second(shape, dtype):
    return pl.pallas_call(
        lambda out: None,
        out_shape=jax.ShapeDtypeStruct(shape, dtype),
        out_specs=HBM,
        compiler_params=PARAMS,
        name="no_second",
    )()


def finish(notes, own, other, second, total, col_table, row_table):
    height, breadth = total.shape
    places, edge = notes.shape[0], second.shape[1]
    components = col_table.shape[1] // LANE
    chips = len(own)
    wide = breadth // edge

    def kernel(*refs):
        words, by_core = refs[0], (refs[1 : 1 + chips], refs[1 + chips : 1 + 2 * chips])
        (by_source, total_in, col_taps, row_taps, out, held, image, padded, stage, result, sems,
         out_sems) = refs[1 + 2 * chips:]
        here = lax.axis_index("patch")
        core, chip = lax.rem(here, CORES), lax.div(here, CORES)
        left_over = words[0, 3]
        for p in range(1, places):
            left_over = left_over + words[p, 3]
        image[...] = total_in[...]

        @pl.when(left_over == 0)
        def _():
            for n in range(CORES):
                for d in range(chips):
                    sender = lax.rem(core + n, CORES)
                    p = lax.rem(chip - d + chips, chips) * CORES + sender
                    label = words[p, 2]

                    @pl.when(words[p, 1] == core)
                    def _(block=by_core[n][d], label=label):
                        spot = spot_of(label, edge, wide)
                        image[spot] = image[spot] + block[...].astype(F32)

        @pl.when(left_over > 0)
        def _():
            def begin(p, carry):
                @pl.when(words[p, 4] >= 0)
                def _():
                    pltpu.make_async_copy(by_source.at[p], held.at[p], sems.at[p]).start()

                return carry

            def add(p, carry):
                @pl.when(words[p, 4] >= 0)
                def _():
                    pltpu.make_async_copy(by_source.at[p], held.at[p], sems.at[p]).wait()
                    spot = spot_of(words[p, 4], edge, wide)
                    image[spot] = image[spot] + held[p].astype(F32)

                return carry

            lax.fori_loop(0, places, begin, 0)
            lax.fori_loop(0, places, add, 0)

        for r in range(0, height, LANE):
            padded[pl.ds(r, LANE), :] = shifted(image[pl.ds(r, LANE), :])
        copies = []
        for j in range(breadth // WINDOW):
            store_strip(result, filter_strip(padded, col_taps, row_taps, stage, j), j)
            spot = (pl.ds(0, height), pl.ds(j * WINDOW, WINDOW))
            copies.append(pltpu.make_async_copy(result.at[spot], out.at[spot], out_sems.at[j]))
            copies[-1].start()
        for copy in copies:
            copy.wait()

    return pl.pallas_call(
        kernel,
        out_shape=jax.ShapeDtypeStruct((height, breadth), F32),
        in_specs=[SMEM] + [VMEM] * (2 * chips) + [HBM] + [VMEM] * 3,
        out_specs=HBM,
        scratch_shapes=[
            pltpu.VMEM((places, edge, edge), BF16),
            pltpu.VMEM((height, breadth), F32),
            pltpu.VMEM((height, breadth + 2 * HALO), BF16),
            pltpu.VMEM((2, components * WINDOW, WINDOW), BF16),
            pltpu.VMEM((height, breadth), F32),
            pltpu.SemaphoreType.DMA((places,)),
            pltpu.SemaphoreType.DMA((breadth // WINDOW,)),
        ],
        compiler_params=PARAMS,
        name="finish",
    )(notes, *own, *other, second, total, col_table, row_table)


def per_device(
    blocks,
    block_patch,
    block_slot,
    block_count,
    template,
    basis_rows,
    basis_cols,
    coeffs,
    psf_rows,
    psf_cols,
):
    n_patch, n_visit = lax.axis_size("patch"), lax.axis_size("visit")
    chips = n_patch // CORES
    side = 4
    assert side * side == n_visit
    pieces, patches = blocks[0, 0], block_patch.reshape(-1)
    slots, count = block_slot.reshape(-1), block_count.reshape(-1)

    def to_chip(d):
        return [(i, (i + CORES * d) % n_patch) for i in range(n_patch)]

    outgoing = pack_main(pieces, patches, slots, count, n_patch)
    arrived = lax.all_to_all(outgoing, "patch", 0, 0, tiled=True)

    def along_x(d):
        return [(i, i // side * side + (i + d) % side) for i in range(n_visit)]

    def along_y(d):
        return [(i, (i + side * d) % n_visit) for i in range(n_visit)]

    rows = template[0]
    near = [rows] + [lax.ppermute(rows, "visit", along_x(d)) for d in range(1, side)]
    near = jnp.concatenate(near, axis=0)
    groups = [near] + [lax.ppermute(near, "visit", along_y(d)) for d in range(1, side)]
    scaled = coeffs[0][:, None] * basis_cols
    me = lax.axis_index("visit").reshape(1).astype(jnp.int32)
    total, col_table, row_table = make_model(
        groups, me, basis_rows.astype(F32), scaled, psf_rows[0].astype(F32),
        psf_cols[0].astype(F32),
    )
    extra = pack_extra(pieces, patches, count, col_table, n_patch)
    edge = pieces.shape[1]
    notes = arrived[:, edge, :NOTE_WORDS].astype(jnp.int32)
    total = add_first(notes, arrived, total)

    def by_source():
        second = pack_second(pieces, patches, count, n_patch)
        return lax.all_to_all(second, "patch", 0, 0, tiled=True)

    def by_chip():
        return no_second((n_patch, edge, edge), pieces.dtype)

    second = lax.cond(jnp.any(notes[:, 3] > 0), by_source, by_chip)
    neighbour = [(i, i ^ 1) for i in range(n_patch)]
    own, other = list(extra), [None] * chips
    near_last = sorted(range(1, chips), key=lambda d: -min(d, chips - d))
    early, last = near_last[:-2], near_last[-2:]
    for d in early:
        own[d] = lax.ppermute(extra[d], "patch", to_chip(d))
    for d in last:
        waiting, _ = lax.optimization_barrier((extra[d], second))
        own[d] = lax.ppermute(waiting, "patch", to_chip(d))
    for d in [0] + early + last:
        own[d], _ = lax.optimization_barrier((own[d], total if d in last else second))
        other[d] = lax.ppermute(own[d], "patch", neighbour)
    filtered = finish(notes, own, other, second, total, col_table, row_table)
    return filtered[None, None]


def solution(mesh):
    placed = (
        P("patch", "visit", None, None, None),
        P("patch", "visit", None, None),
        P("patch", "visit", None),
        P("patch", "visit"),
        P("patch", "visit", None),
        P(),
        P(),
        P("visit", None),
        P("visit", None, None),
        P("visit", None, None),
    )
    return jax.shard_map(
        per_device,
        mesh=mesh,
        in_specs=placed,
        out_specs=P("patch", "visit", None, None),
        check_vma=False,
    )
```

```python
import jax
import jax.numpy as jnp
from jax import lax
from jax.experimental import pallas as pl
from jax.experimental.pallas import tpu as pltpu
from jax.sharding import PartitionSpec as P

CORES = 2
NOTE_ROWS = 16
NOTE_WORDS = 8
LANE = 128
HALO = 64
WINDOW = 256
LAP = 16
F32 = jnp.float32
BF16 = jnp.bfloat16
PARAMS = pltpu.CompilerParams(vmem_limit_bytes=48 * 1024 * 1024)
SMEM = pl.BlockSpec(memory_space=pltpu.SMEM)
VMEM = pl.BlockSpec(memory_space=pltpu.VMEM)
HBM = pl.BlockSpec(memory_space=pltpu.HBM)


def scan_entries(lists, first, second, extra, chips, here):
    patch, count, entries = lists
    for q in range(first.shape[0]):
        first[q] = -1
        second[q] = -1
    for d in range(chips):
        extra[d] = -1

    def visit(i, left_over):
        q = patch[i]
        again = first[q] >= 0
        d = lax.rem(lax.div(q, CORES) - here + chips, chips)
        taken = extra[d] >= 0

        @pl.when(jnp.logical_not(again))
        def _():
            first[q] = i

        @pl.when(again)
        def _():
            second[q] = i

        @pl.when(jnp.logical_and(again, jnp.logical_not(taken)))
        def _():
            extra[d] = i

        return left_over + jnp.logical_and(again, taken).astype(jnp.int32)

    return lax.fori_loop(0, jnp.minimum(count[0], entries), visit, jnp.int32(0))


def copy_entry(blocks, i, target):
    @pl.when(i >= 0)
    def _():
        target[...] = blocks[jnp.maximum(i, 0)]


def list_scratch(places):
    return [
        pltpu.SMEM((places,), jnp.int32),
        pltpu.SMEM((places,), jnp.int32),
        pltpu.SMEM((places // CORES,), jnp.int32),
    ]


def pack_extra_kernel(patch, count, blocks, after, *refs):
    chips = len(refs) - 3
    outs = refs[:chips]
    first, second, extra = refs[chips:]
    here = lax.div(lax.axis_index("patch"), CORES)
    scan_entries((patch, count, blocks.shape[0]), first, second, extra, chips, here)
    for d in range(chips):
        copy_entry(blocks, extra[d], outs[d])


def pack_extra(blocks, block_patch, block_count, after, places):
    edge = blocks.shape[1]
    chips = places // CORES
    return pl.pallas_call(
        pack_extra_kernel,
        out_shape=(jax.ShapeDtypeStruct((edge, edge), blocks.dtype),) * chips,
        in_specs=[SMEM, SMEM, VMEM, VMEM],
        out_specs=(VMEM,) * chips,
        scratch_shapes=list_scratch(places),
        compiler_params=PARAMS,
        name="pack_extra",
    )(block_patch, block_count, blocks, after)


def pack_main_kernel(patch, slot, count, blocks, outgoing, first, second, extra):
    places = outgoing.shape[0]
    edge = blocks.shape[1]
    chips = places // CORES
    here = lax.div(lax.axis_index("patch"), CORES)
    left_over = scan_entries((patch, count, blocks.shape[0]), first, second, extra, chips, here)
    lane = lax.broadcasted_iota(jnp.int32, (NOTE_ROWS, edge), 1)
    for q in range(places):
        i, j = first[q], second[q]
        e = extra[lax.rem(q // CORES - here + chips, chips)]
        copy_entry(blocks, i, outgoing.at[q, pl.ds(0, edge)])
        words = (
            jnp.where(i >= 0, slot[jnp.maximum(i, 0)], -1),
            jnp.where(e >= 0, lax.rem(patch[jnp.maximum(e, 0)], CORES), -1),
            jnp.where(e >= 0, slot[jnp.maximum(e, 0)], -1),
            left_over,
            jnp.where(j >= 0, slot[jnp.maximum(j, 0)], -1),
        )
        row = jnp.zeros((NOTE_ROWS, edge), jnp.int32)
        for n, word in enumerate(words):
            row = jnp.where(lane == n, word, row)
        outgoing[q, pl.ds(edge, NOTE_ROWS), :] = row.astype(F32).astype(outgoing.dtype)


def pack_main(blocks, block_patch, block_slot, block_count, places):
    edge = blocks.shape[1]
    return pl.pallas_call(
        pack_main_kernel,
        out_shape=jax.ShapeDtypeStruct((places, edge + NOTE_ROWS, edge), blocks.dtype),
        in_specs=[SMEM, SMEM, SMEM, VMEM],
        out_specs=VMEM,
        scratch_shapes=list_scratch(places),
        compiler_params=PARAMS,
        name="pack_main",
    )(block_patch, block_slot, block_count, blocks)


def pack_second_kernel(patch, count, blocks, outgoing, first, second, extra):
    places = outgoing.shape[0]
    here = lax.div(lax.axis_index("patch"), CORES)
    scan_entries((patch, count, blocks.shape[0]), first, second, extra, places // CORES, here)
    for q in range(places):
        copy_entry(blocks, second[q], outgoing.at[q])


def pack_second(blocks, block_patch, block_count, places):
    edge = blocks.shape[1]
    return pl.pallas_call(
        pack_second_kernel,
        out_shape=jax.ShapeDtypeStruct((places, edge, edge), blocks.dtype),
        in_specs=[SMEM, SMEM, VMEM],
        out_specs=VMEM,
        scratch_shapes=list_scratch(places),
        compiler_params=PARAMS,
        name="pack_second",
    )(block_patch, block_count, blocks)


def fill_band(table, taps, index, row0, col0, height, breadth, sign, base):
    length = taps.shape[1]
    for r in range(0, height, 16):
        rows = lax.broadcasted_iota(jnp.int32, (16, breadth), 0)
        cols = lax.broadcasted_iota(jnp.int32, (16, breadth), 1)
        offset = sign * (rows - cols) + (sign * r + base)
        values = jnp.zeros((16, breadth), F32)
        for u in range(length):
            values = jnp.where(offset == u, taps[index, u], values)
        table[pl.ds(row0 + r, 16), pl.ds(col0, breadth)] = values.astype(table.dtype)


def fill_tables(col_table, row_table, col_taps, row_taps):
    half = col_taps.shape[1] // 2
    for k in range(col_taps.shape[0]):
        fill_band(col_table, col_taps, k, 0, k * LANE, WINDOW, LANE, 1, half - HALO)
        for w in range(2):
            fill_band(
                row_table.at[w], row_taps, k, 0, k * WINDOW, WINDOW + LAP, WINDOW, -1,
                half + w * LAP,
            )


def shifted(values):
    rows = values.shape[0]
    edge = jnp.zeros((rows, HALO), F32)
    return jnp.concatenate([edge, values, edge], axis=1).astype(BF16)


def filter_strip(padded, col_table, row_table, stage, strip):
    count = col_table.shape[1] // LANE
    for h in range(2):
        start = strip * WINDOW + h * LANE
        if not isinstance(start, int):
            start = pl.multiple_of(start, LANE)
        for w in range(2):
            across = jnp.dot(
                padded[pl.ds(w * WINDOW, WINDOW), pl.ds(start, WINDOW)],
                col_table[...],
                preferred_element_type=F32,
            ).astype(BF16)
            for k in range(count):
                stage[w, pl.ds(k * WINDOW, WINDOW), pl.ds(h * LANE, LANE)] = across[
                    :, k * LANE : (k + 1) * LANE
                ]
    top = jnp.dot(row_table[0], stage[0], preferred_element_type=F32)
    low = jnp.dot(row_table[1], stage[1], preferred_element_type=F32)
    cut = WINDOW - LAP
    return top[:cut], top[cut:] + low[: 2 * LAP], low[2 * LAP :]


def store_strip(target, parts, strip):
    start = strip * WINDOW
    if not isinstance(start, int):
        start = pl.multiple_of(start, LANE)
    row = 0
    for part in parts:
        target[pl.ds(row, part.shape[0]), pl.ds(start, WINDOW)] = part
        row += part.shape[0]


def make_model(pieces, me, basis_rows, scaled, psf_rows, psf_cols):
    parts = len(pieces)
    group_rows, breadth = pieces[0].shape
    local_rows = group_rows // parts
    height = parts * group_rows
    basis, components = basis_rows.shape[0], psf_rows.shape[0]

    def kernel(*refs):
        sources = refs[:parts]
        (position, basis_taps, scaled_taps, psf_row_taps, psf_col_taps, less, psf_col_table,
         psf_row_table, padded, col_table, row_table, stage) = refs[parts:]
        fill_tables(col_table, row_table, basis_taps, scaled_taps)
        y, x = lax.div(position[0], parts), lax.rem(position[0], parts)
        for dy, source in enumerate(sources):
            for dx in range(parts):
                owner = lax.rem(y - dy + parts, parts) * parts + lax.rem(x - dx + parts, parts)
                start = pl.multiple_of(owner * local_rows, local_rows)
                padded[pl.ds(start, local_rows), :] = shifted(
                    source[pl.ds(dx * local_rows, local_rows), :].astype(F32)
                )

        def strip(j, carry):
            parts = filter_strip(padded, col_table, row_table, stage, j)
            store_strip(less, [-part for part in parts], j)
            return carry

        lax.fori_loop(0, breadth // WINDOW, strip, 0)
        fill_tables(psf_col_table, psf_row_table, psf_row_taps, psf_col_taps)

    return pl.pallas_call(
        kernel,
        out_shape=(
            jax.ShapeDtypeStruct((height, breadth), F32),
            jax.ShapeDtypeStruct((WINDOW, components * LANE), BF16),
            jax.ShapeDtypeStruct((2, WINDOW + LAP, components * WINDOW), BF16),
        ),
        in_specs=[VMEM] * parts + [SMEM] * 5,
        out_specs=(VMEM, VMEM, VMEM),
        scratch_shapes=[
            pltpu.VMEM((height, breadth + 2 * HALO), BF16),
            pltpu.VMEM((WINDOW, basis * LANE), BF16),
            pltpu.VMEM((2, WINDOW + LAP, basis * WINDOW), BF16),
            pltpu.VMEM((2, basis * WINDOW, WINDOW), BF16),
        ],
        compiler_params=PARAMS,
        name="model",
    )(*pieces, me, basis_rows, scaled, psf_rows, psf_cols)


def spot_of(label, edge, wide):
    row = pl.multiple_of(lax.div(label, wide) * edge, edge)
    col = pl.multiple_of(lax.rem(label, wide) * edge, edge)
    return pl.ds(row, edge), pl.ds(col, edge)


def add_first(notes, main, model_negative):
    height, breadth = model_negative.shape
    places, edge = main.shape[0], main.shape[2]

    def kernel(words, blocks, less, total):
        total[...] = less[...]

        def step(p, carry):
            label = words[p, 0]

            @pl.when(label >= 0)
            def _():
                spot = spot_of(label, edge, breadth // edge)
                total[spot] = total[spot] + blocks[p, pl.ds(0, edge), :].astype(F32)

            return carry

        lax.fori_loop(0, places, step, 0)

    return pl.pallas_call(
        kernel,
        out_shape=jax.ShapeDtypeStruct((height, breadth), F32),
        in_specs=[SMEM, VMEM, VMEM],
        out_specs=VMEM,
        compiler_params=PARAMS,
        name="add_first",
    )(notes, main, model_negative)


def no_second(shape, dtype):
    return pl.pallas_call(
        lambda out: None,
        out_shape=jax.ShapeDtypeStruct(shape, dtype),
        out_specs=HBM,
        compiler_params=PARAMS,
        name="no_second",
    )()


def finish(notes, own, other, second, total, col_table, row_table):
    height, breadth = total.shape
    places, edge = notes.shape[0], second.shape[1]
    components = col_table.shape[1] // LANE
    chips = len(own)
    wide = breadth // edge

    def kernel(*refs):
        words, mine = refs[0], refs[1 : 1 + chips]
        theirs = [None] * chips
        for (group, _), handed in zip(other, refs[1 + chips :]):
            for n, d in enumerate(group):
                theirs[d] = handed.at[n]
        by_core = (mine, theirs)
        (by_source, total_in, col_taps, row_taps, out, held, image, padded, stage, result, sems,
         out_sems) = refs[1 + chips + len(other):]
        here = lax.axis_index("patch")
        core, chip = lax.rem(here, CORES), lax.div(here, CORES)
        left_over = words[0, 3]
        for p in range(1, places):
            left_over = left_over + words[p, 3]
        image[...] = total_in[...]

        @pl.when(left_over == 0)
        def _():
            for n in range(CORES):
                for d in range(chips):
                    sender = lax.rem(core + n, CORES)
                    p = lax.rem(chip - d + chips, chips) * CORES + sender
                    label = words[p, 2]

                    @pl.when(words[p, 1] == core)
                    def _(block=by_core[n][d], label=label):
                        spot = spot_of(label, edge, wide)
                        image[spot] = image[spot] + block[...].astype(F32)

        @pl.when(left_over > 0)
        def _():
            def begin(p, carry):
                @pl.when(words[p, 4] >= 0)
                def _():
                    pltpu.make_async_copy(by_source.at[p], held.at[p], sems.at[p]).start()

                return carry

            def add(p, carry):
                @pl.when(words[p, 4] >= 0)
                def _():
                    pltpu.make_async_copy(by_source.at[p], held.at[p], sems.at[p]).wait()
                    spot = spot_of(words[p, 4], edge, wide)
                    image[spot] = image[spot] + held[p].astype(F32)

                return carry

            lax.fori_loop(0, places, begin, 0)
            lax.fori_loop(0, places, add, 0)

        for r in range(0, height, LANE):
            padded[pl.ds(r, LANE), :] = shifted(image[pl.ds(r, LANE), :])
        copies = []
        for j in range(breadth // WINDOW):
            store_strip(result, filter_strip(padded, col_taps, row_taps, stage, j), j)
            spot = (pl.ds(0, height), pl.ds(j * WINDOW, WINDOW))
            copies.append(pltpu.make_async_copy(result.at[spot], out.at[spot], out_sems.at[j]))
            copies[-1].start()
        for copy in copies:
            copy.wait()

    return pl.pallas_call(
        kernel,
        out_shape=jax.ShapeDtypeStruct((height, breadth), F32),
        in_specs=[SMEM] + [VMEM] * (chips + len(other)) + [HBM] + [VMEM] * 3,
        out_specs=HBM,
        scratch_shapes=[
            pltpu.VMEM((places, edge, edge), BF16),
            pltpu.VMEM((height, breadth), F32),
            pltpu.VMEM((height, breadth + 2 * HALO), BF16),
            pltpu.VMEM((2, components * WINDOW, WINDOW), BF16),
            pltpu.VMEM((height, breadth), F32),
            pltpu.SemaphoreType.DMA((places,)),
            pltpu.SemaphoreType.DMA((breadth // WINDOW,)),
        ],
        compiler_params=PARAMS,
        name="finish",
    )(notes, *own, *[handed for _, handed in other], second, total, col_table, row_table)


def per_device(
    blocks,
    block_patch,
    block_slot,
    block_count,
    template,
    basis_rows,
    basis_cols,
    coeffs,
    psf_rows,
    psf_cols,
):
    n_patch, n_visit = lax.axis_size("patch"), lax.axis_size("visit")
    chips = n_patch // CORES
    side = 4
    assert side * side == n_visit
    pieces, patches = blocks[0, 0], block_patch.reshape(-1)
    slots, count = block_slot.reshape(-1), block_count.reshape(-1)

    def to_chip(d):
        return [(i, (i + CORES * d) % n_patch) for i in range(n_patch)]

    outgoing = pack_main(pieces, patches, slots, count, n_patch)
    arrived = lax.all_to_all(outgoing, "patch", 0, 0, tiled=True)

    def along_x(d):
        return [(i, i // side * side + (i + d) % side) for i in range(n_visit)]

    def along_y(d):
        return [(i, (i + side * d) % n_visit) for i in range(n_visit)]

    rows = template[0]
    near = [rows] + [lax.ppermute(rows, "visit", along_x(d)) for d in range(1, side)]
    near = jnp.concatenate(near, axis=0)
    groups = [near] + [lax.ppermute(near, "visit", along_y(d)) for d in range(1, side)]
    scaled = coeffs[0][:, None] * basis_cols
    me = lax.axis_index("visit").reshape(1).astype(jnp.int32)
    total, col_table, row_table = make_model(
        groups, me, basis_rows.astype(F32), scaled, psf_rows[0].astype(F32),
        psf_cols[0].astype(F32),
    )
    extra = pack_extra(pieces, patches, count, col_table, n_patch)
    edge = pieces.shape[1]
    notes = arrived[:, edge, :NOTE_WORDS].astype(jnp.int32)
    total = add_first(notes, arrived, total)

    def by_source():
        second = pack_second(pieces, patches, count, n_patch)
        return lax.all_to_all(second, "patch", 0, 0, tiled=True)

    def by_chip():
        return no_second((n_patch, edge, edge), pieces.dtype)

    second = lax.cond(jnp.any(notes[:, 3] > 0), by_source, by_chip)
    neighbour = [(i, i ^ 1) for i in range(n_patch)]
    own = list(extra)
    near_last = sorted(range(1, chips), key=lambda d: -min(d, chips - d))
    early, last = near_last[:-2], near_last[-2:]
    for d in early:
        own[d] = lax.ppermute(extra[d], "patch", to_chip(d))
    for d in last:
        waiting, _ = lax.optimization_barrier((extra[d], second))
        own[d] = lax.ppermute(waiting, "patch", to_chip(d))
    other = []
    for group, ready in (([0] + early[:3], second), (early[3:] + last, total)):
        for d in group:
            own[d], _ = lax.optimization_barrier((own[d], ready))
        handed = jnp.stack([own[d] for d in group])
        other.append((group, lax.ppermute(handed, "patch", neighbour)))
    filtered = finish(notes, own, other, second, total, col_table, row_table)
    return filtered[None, None]


def solution(mesh):
    placed = (
        P("patch", "visit", None, None, None),
        P("patch", "visit", None, None),
        P("patch", "visit", None),
        P("patch", "visit"),
        P("patch", "visit", None),
        P(),
        P(),
        P("visit", None),
        P("visit", None, None),
        P("visit", None, None),
    )
    return jax.shard_map(
        per_device,
        mesh=mesh,
        in_specs=placed,
        out_specs=P("patch", "visit", None, None),
        check_vma=False,
    )
```

```python
import jax
import jax.numpy as jnp
from jax import lax
from jax.experimental import pallas as pl
from jax.experimental.pallas import tpu as pltpu
from jax.sharding import PartitionSpec as P

CORES = 2
NOTE_ROWS = 16
NOTE_WORDS = 8
LANE = 128
HALO = 64
WINDOW = 256
LAP = 16
F32 = jnp.float32
BF16 = jnp.bfloat16
PARAMS = pltpu.CompilerParams(vmem_limit_bytes=48 * 1024 * 1024)
SMEM = pl.BlockSpec(memory_space=pltpu.SMEM)
VMEM = pl.BlockSpec(memory_space=pltpu.VMEM)
HBM = pl.BlockSpec(memory_space=pltpu.HBM)


def scan_entries(lists, first, second, extra, chips, here):
    patch, count, entries = lists
    for q in range(first.shape[0]):
        first[q] = -1
        second[q] = -1
    for d in range(chips):
        extra[d] = -1

    def visit(i, left_over):
        q = patch[i]
        again = first[q] >= 0
        d = lax.rem(lax.div(q, CORES) - here + chips, chips)
        taken = extra[d] >= 0

        @pl.when(jnp.logical_not(again))
        def _():
            first[q] = i

        @pl.when(again)
        def _():
            second[q] = i

        @pl.when(jnp.logical_and(again, jnp.logical_not(taken)))
        def _():
            extra[d] = i

        return left_over + jnp.logical_and(again, taken).astype(jnp.int32)

    return lax.fori_loop(0, jnp.minimum(count[0], entries), visit, jnp.int32(0))


def copy_entry(blocks, i, target):
    @pl.when(i >= 0)
    def _():
        target[...] = blocks[jnp.maximum(i, 0)]


def list_scratch(places):
    return [
        pltpu.SMEM((places,), jnp.int32),
        pltpu.SMEM((places,), jnp.int32),
        pltpu.SMEM((places // CORES,), jnp.int32),
    ]


def pack_extra_kernel(patch, count, blocks, after, *refs):
    chips = len(refs) - 3
    outs = refs[:chips]
    first, second, extra = refs[chips:]
    here = lax.div(lax.axis_index("patch"), CORES)
    scan_entries((patch, count, blocks.shape[0]), first, second, extra, chips, here)
    for d in range(chips):
        copy_entry(blocks, extra[d], outs[d])


def pack_extra(blocks, block_patch, block_count, after, places):
    edge = blocks.shape[1]
    chips = places // CORES
    return pl.pallas_call(
        pack_extra_kernel,
        out_shape=(jax.ShapeDtypeStruct((edge, edge), blocks.dtype),) * chips,
        in_specs=[SMEM, SMEM, VMEM, VMEM],
        out_specs=(VMEM,) * chips,
        scratch_shapes=list_scratch(places),
        compiler_params=PARAMS,
        name="pack_extra",
    )(block_patch, block_count, blocks, after)


def pack_main_kernel(patch, slot, count, blocks, outgoing, first, second, extra):
    places = outgoing.shape[0]
    edge = blocks.shape[1]
    chips = places // CORES
    here = lax.div(lax.axis_index("patch"), CORES)
    left_over = scan_entries((patch, count, blocks.shape[0]), first, second, extra, chips, here)
    lane = lax.broadcasted_iota(jnp.int32, (NOTE_ROWS, edge), 1)
    for q in range(places):
        i, j = first[q], second[q]
        e = extra[lax.rem(q // CORES - here + chips, chips)]
        copy_entry(blocks, i, outgoing.at[q, pl.ds(0, edge)])
        words = (
            jnp.where(i >= 0, slot[jnp.maximum(i, 0)], -1),
            jnp.where(e >= 0, lax.rem(patch[jnp.maximum(e, 0)], CORES), -1),
            jnp.where(e >= 0, slot[jnp.maximum(e, 0)], -1),
            left_over,
            jnp.where(j >= 0, slot[jnp.maximum(j, 0)], -1),
        )
        row = jnp.zeros((NOTE_ROWS, edge), jnp.int32)
        for n, word in enumerate(words):
            row = jnp.where(lane == n, word, row)
        outgoing[q, pl.ds(edge, NOTE_ROWS), :] = row.astype(F32).astype(outgoing.dtype)


def pack_main(blocks, block_patch, block_slot, block_count, places):
    edge = blocks.shape[1]
    return pl.pallas_call(
        pack_main_kernel,
        out_shape=jax.ShapeDtypeStruct((places, edge + NOTE_ROWS, edge), blocks.dtype),
        in_specs=[SMEM, SMEM, SMEM, VMEM],
        out_specs=VMEM,
        scratch_shapes=list_scratch(places),
        compiler_params=PARAMS,
        name="pack_main",
    )(block_patch, block_slot, block_count, blocks)


def pack_second_kernel(patch, count, blocks, outgoing, first, second, extra):
    places = outgoing.shape[0]
    here = lax.div(lax.axis_index("patch"), CORES)
    scan_entries((patch, count, blocks.shape[0]), first, second, extra, places // CORES, here)
    for q in range(places):
        copy_entry(blocks, second[q], outgoing.at[q])


def pack_second(blocks, block_patch, block_count, places):
    edge = blocks.shape[1]
    return pl.pallas_call(
        pack_second_kernel,
        out_shape=jax.ShapeDtypeStruct((places, edge, edge), blocks.dtype),
        in_specs=[SMEM, SMEM, VMEM],
        out_specs=VMEM,
        scratch_shapes=list_scratch(places),
        compiler_params=PARAMS,
        name="pack_second",
    )(block_patch, block_count, blocks)


def fill_band(table, taps, index, row0, col0, height, breadth, sign, base):
    length = taps.shape[1]
    for r in range(0, height, 16):
        rows = lax.broadcasted_iota(jnp.int32, (16, breadth), 0)
        cols = lax.broadcasted_iota(jnp.int32, (16, breadth), 1)
        offset = sign * (rows - cols) + (sign * r + base)
        values = jnp.zeros((16, breadth), F32)
        for u in range(length):
            values = jnp.where(offset == u, taps[index, u], values)
        table[pl.ds(row0 + r, 16), pl.ds(col0, breadth)] = values.astype(table.dtype)


def fill_tables(col_table, row_table, col_taps, row_taps):
    half = col_taps.shape[1] // 2
    for k in range(col_taps.shape[0]):
        fill_band(col_table, col_taps, k, 0, k * LANE, WINDOW, LANE, 1, half - HALO)
        for w in range(2):
            fill_band(
                row_table.at[w], row_taps, k, 0, k * WINDOW, WINDOW + LAP, WINDOW, -1,
                half + w * LAP,
            )


def shifted(values):
    rows = values.shape[0]
    edge = jnp.zeros((rows, HALO), F32)
    return jnp.concatenate([edge, values, edge], axis=1).astype(BF16)


def filter_strip(padded, col_table, row_table, stage, strip):
    count = col_table.shape[1] // LANE
    for h in range(2):
        start = strip * WINDOW + h * LANE
        if not isinstance(start, int):
            start = pl.multiple_of(start, LANE)
        for w in range(2):
            across = jnp.dot(
                padded[pl.ds(w * WINDOW, WINDOW), pl.ds(start, WINDOW)],
                col_table[...],
                preferred_element_type=F32,
            ).astype(BF16)
            for k in range(count):
                stage[w, pl.ds(k * WINDOW, WINDOW), pl.ds(h * LANE, LANE)] = across[
                    :, k * LANE : (k + 1) * LANE
                ]
    top = jnp.dot(row_table[0], stage[0], preferred_element_type=F32)
    low = jnp.dot(row_table[1], stage[1], preferred_element_type=F32)
    cut = WINDOW - LAP
    return top[:cut], top[cut:] + low[: 2 * LAP], low[2 * LAP :]


def store_strip(target, parts, strip):
    start = strip * WINDOW
    if not isinstance(start, int):
        start = pl.multiple_of(start, LANE)
    row = 0
    for part in parts:
        target[pl.ds(row, part.shape[0]), pl.ds(start, WINDOW)] = part
        row += part.shape[0]


def make_model(pieces, me, basis_rows, scaled, psf_rows, psf_cols):
    parts = len(pieces)
    group_rows, breadth = pieces[0].shape
    local_rows = group_rows // parts
    height = parts * group_rows
    basis, components = basis_rows.shape[0], psf_rows.shape[0]

    def kernel(*refs):
        sources = refs[:parts]
        (position, basis_taps, scaled_taps, psf_row_taps, psf_col_taps, less, psf_col_table,
         psf_row_table, padded, col_table, row_table, stage) = refs[parts:]
        fill_tables(col_table, row_table, basis_taps, scaled_taps)
        y, x = lax.div(position[0], parts), lax.rem(position[0], parts)
        for dy, source in enumerate(sources):
            for dx in range(parts):
                owner = lax.rem(y - dy + parts, parts) * parts + lax.rem(x - dx + parts, parts)
                start = pl.multiple_of(owner * local_rows, local_rows)
                padded[pl.ds(start, local_rows), :] = shifted(
                    source[pl.ds(dx * local_rows, local_rows), :].astype(F32)
                )

        def strip(j, carry):
            parts = filter_strip(padded, col_table, row_table, stage, j)
            store_strip(less, [-part for part in parts], j)
            return carry

        lax.fori_loop(0, breadth // WINDOW, strip, 0)
        fill_tables(psf_col_table, psf_row_table, psf_row_taps, psf_col_taps)

    return pl.pallas_call(
        kernel,
        out_shape=(
            jax.ShapeDtypeStruct((height, breadth), F32),
            jax.ShapeDtypeStruct((WINDOW, components * LANE), BF16),
            jax.ShapeDtypeStruct((2, WINDOW + LAP, components * WINDOW), BF16),
        ),
        in_specs=[VMEM] * parts + [SMEM] * 5,
        out_specs=(VMEM, VMEM, VMEM),
        scratch_shapes=[
            pltpu.VMEM((height, breadth + 2 * HALO), BF16),
            pltpu.VMEM((WINDOW, basis * LANE), BF16),
            pltpu.VMEM((2, WINDOW + LAP, basis * WINDOW), BF16),
            pltpu.VMEM((2, basis * WINDOW, WINDOW), BF16),
        ],
        compiler_params=PARAMS,
        name="model",
    )(*pieces, me, basis_rows, scaled, psf_rows, psf_cols)


def spot_of(label, edge, wide):
    row = pl.multiple_of(lax.div(label, wide) * edge, edge)
    col = pl.multiple_of(lax.rem(label, wide) * edge, edge)
    return pl.ds(row, edge), pl.ds(col, edge)


def add_first(notes, main, model_negative):
    height, breadth = model_negative.shape
    places, edge = main.shape[0], main.shape[2]

    def kernel(words, blocks, less, total):
        total[...] = less[...]

        def step(p, carry):
            label = words[p, 0]

            @pl.when(label >= 0)
            def _():
                spot = spot_of(label, edge, breadth // edge)
                total[spot] = total[spot] + blocks[p, pl.ds(0, edge), :].astype(F32)

            return carry

        lax.fori_loop(0, places, step, 0)

    return pl.pallas_call(
        kernel,
        out_shape=jax.ShapeDtypeStruct((height, breadth), F32),
        in_specs=[SMEM, VMEM, VMEM],
        out_specs=VMEM,
        compiler_params=PARAMS,
        name="add_first",
    )(notes, main, model_negative)


def no_second(shape, dtype):
    return pl.pallas_call(
        lambda out: None,
        out_shape=jax.ShapeDtypeStruct(shape, dtype),
        out_specs=HBM,
        compiler_params=PARAMS,
        name="no_second",
    )()


def finish(notes, own, other, second, total, col_table, row_table):
    height, breadth = total.shape
    places, edge = notes.shape[0], second.shape[1]
    components = col_table.shape[1] // LANE
    chips = len(own)
    wide = breadth // edge

    def kernel(*refs):
        words, by_core = refs[0], (refs[1 : 1 + chips], refs[1 + chips : 1 + 2 * chips])
        (by_source, total_in, col_taps, row_taps, out, held, image, padded, stage, result, sems,
         out_sems) = refs[1 + 2 * chips:]
        here = lax.axis_index("patch")
        core, chip = lax.rem(here, CORES), lax.div(here, CORES)
        left_over = words[0, 3]
        for p in range(1, places):
            left_over = left_over + words[p, 3]
        image[...] = total_in[...]

        @pl.when(left_over == 0)
        def _():
            for n in range(CORES):
                for d in range(chips):
                    sender = lax.rem(core + n, CORES)
                    p = lax.rem(chip - d + chips, chips) * CORES + sender
                    label = words[p, 2]

                    @pl.when(words[p, 1] == core)
                    def _(block=by_core[n][d], label=label):
                        spot = spot_of(label, edge, wide)
                        image[spot] = image[spot] + block[...].astype(F32)

        @pl.when(left_over > 0)
        def _():
            def begin(p, carry):
                @pl.when(words[p, 4] >= 0)
                def _():
                    pltpu.make_async_copy(by_source.at[p], held.at[p], sems.at[p]).start()

                return carry

            def add(p, carry):
                @pl.when(words[p, 4] >= 0)
                def _():
                    pltpu.make_async_copy(by_source.at[p], held.at[p], sems.at[p]).wait()
                    spot = spot_of(words[p, 4], edge, wide)
                    image[spot] = image[spot] + held[p].astype(F32)

                return carry

            lax.fori_loop(0, places, begin, 0)
            lax.fori_loop(0, places, add, 0)

        for r in range(0, height, LANE):
            padded[pl.ds(r, LANE), :] = shifted(image[pl.ds(r, LANE), :])
        copies = []
        for j in range(breadth // WINDOW):
            store_strip(result, filter_strip(padded, col_taps, row_taps, stage, j), j)
            spot = (pl.ds(0, height), pl.ds(j * WINDOW, WINDOW))
            copies.append(pltpu.make_async_copy(result.at[spot], out.at[spot], out_sems.at[j]))
            copies[-1].start()
        for copy in copies:
            copy.wait()

    return pl.pallas_call(
        kernel,
        out_shape=jax.ShapeDtypeStruct((height, breadth), F32),
        in_specs=[SMEM] + [VMEM] * (2 * chips) + [HBM] + [VMEM] * 3,
        out_specs=HBM,
        scratch_shapes=[
            pltpu.VMEM((places, edge, edge), BF16),
            pltpu.VMEM((height, breadth), F32),
            pltpu.VMEM((height, breadth + 2 * HALO), BF16),
            pltpu.VMEM((2, components * WINDOW, WINDOW), BF16),
            pltpu.VMEM((height, breadth), F32),
            pltpu.SemaphoreType.DMA((places,)),
            pltpu.SemaphoreType.DMA((breadth // WINDOW,)),
        ],
        compiler_params=PARAMS,
        name="finish",
    )(notes, *own, *other, second, total, col_table, row_table)


def per_device(
    blocks,
    block_patch,
    block_slot,
    block_count,
    template,
    basis_rows,
    basis_cols,
    coeffs,
    psf_rows,
    psf_cols,
):
    n_patch, n_visit = lax.axis_size("patch"), lax.axis_size("visit")
    chips = n_patch // CORES
    side = 4
    assert side * side == n_visit
    pieces, patches = blocks[0, 0], block_patch.reshape(-1)
    slots, count = block_slot.reshape(-1), block_count.reshape(-1)

    def to_chip(d):
        return [(i, (i + CORES * d) % n_patch) for i in range(n_patch)]

    outgoing = pack_main(pieces, patches, slots, count, n_patch)
    arrived = lax.all_to_all(outgoing, "patch", 0, 0, tiled=True)

    def along_x(d):
        return [(i, i // side * side + (i + d) % side) for i in range(n_visit)]

    def along_y(d):
        return [(i, (i + side * d) % n_visit) for i in range(n_visit)]

    rows = template[0]
    near = [rows] + [lax.ppermute(rows, "visit", along_x(d)) for d in range(1, side)]
    near = jnp.concatenate(near, axis=0)
    groups = [near] + [lax.ppermute(near, "visit", along_y(d)) for d in range(1, side)]
    scaled = coeffs[0][:, None] * basis_cols
    me = lax.axis_index("visit").reshape(1).astype(jnp.int32)
    total, col_table, row_table = make_model(
        groups, me, basis_rows.astype(F32), scaled, psf_rows[0].astype(F32),
        psf_cols[0].astype(F32),
    )
    extra = pack_extra(pieces, patches, count, groups[-1], n_patch)
    edge = pieces.shape[1]
    notes = arrived[:, edge, :NOTE_WORDS].astype(jnp.int32)
    total = add_first(notes, arrived, total)

    def by_source():
        second = pack_second(pieces, patches, count, n_patch)
        return lax.all_to_all(second, "patch", 0, 0, tiled=True)

    def by_chip():
        return no_second((n_patch, edge, edge), pieces.dtype)

    second = lax.cond(jnp.any(notes[:, 3] > 0), by_source, by_chip)
    neighbour = [(i, i ^ 1) for i in range(n_patch)]
    own, other = list(extra), [None] * chips
    near_last = sorted(range(1, chips), key=lambda d: -min(d, chips - d))
    early, last = near_last[:-2], near_last[-2:]
    for d in early:
        own[d] = lax.ppermute(extra[d], "patch", to_chip(d))
    for d in last:
        waiting, _ = lax.optimization_barrier((extra[d], second))
        own[d] = lax.ppermute(waiting, "patch", to_chip(d))
    for d in [0] + early + last:
        own[d], _ = lax.optimization_barrier((own[d], total if d in last else second))
        other[d] = lax.ppermute(own[d], "patch", neighbour)
    filtered = finish(notes, own, other, second, total, col_table, row_table)
    return filtered[None, None]


def solution(mesh):
    placed = (
        P("patch", "visit", None, None, None),
        P("patch", "visit", None, None),
        P("patch", "visit", None),
        P("patch", "visit"),
        P("patch", "visit", None),
        P(),
        P(),
        P("visit", None),
        P("visit", None, None),
        P("visit", None, None),
    )
    return jax.shard_map(
        per_device,
        mesh=mesh,
        in_specs=placed,
        out_specs=P("patch", "visit", None, None),
        check_vma=False,
    )
```
